512 devices in a mesh: seq: 64 (over z, y_lo, core), grp: 8 (over x, y_hi).
Axes of the slice: x: 4, y: 4 (y_hi: 2, y_lo: 2; y = y_hi * 2 + y_lo), z: 16, core: 2. Of those that a mesh axis runs over, the one named last changes fastest.
Arguments:
- conditioning: bfloat16 [32, 3072], replicated, may hold values from -6 to 6
- mod_weight: bfloat16 [3072, 6144], P(None, ('seq', 'grp')), may hold values from -0.109375 to 0.109375
- mod_bias: float32 [6144], P(('seq', 'grp')), may hold values from -12 to 12
- hidden: bfloat16 [32, 4096, 3072], P('grp', 'seq'), may hold values from -6 to 6
- proj_weight: bfloat16 [3072, 64], replicated, may hold values from -0.109375 to 0.109375
- proj_bias: float32 [64], replicated, may hold values from -3 to 3
- noisy_latent: bfloat16 [32, 128, 128, 16], P('grp', 'seq'), may hold values from -64 to 64
- in_weight: bfloat16 [144, 512], replicated, may hold values from -0.5 to 0.5
- in_bias: float32 [512], replicated, may hold values from -3 to 3
- norm_gain: float32 [512], replicated, may hold values from 0.1 to 1.9
- norm_shift: float32 [512], replicated, may hold values from -3 to 3
- conv_weight: bfloat16 [4608, 512], P('seq'), may hold values from -0.09375 to 0.09375
- conv_bias: float32 [512], replicated, may hold values from -3 to 3
Outputs:
- decoded: bfloat16 [32, 128, 128, 512], P('grp', 'seq')
The draws below stay inside these ranges and needn't reach their ends.
All inputs are finite; a program needn't handle non-finite values.
Results may differ from the reference program's by a relative error of at most 0.01.
Values may be sent and summed in bfloat16 or wider, within the bound.
A program may use at most 64 MiB of HBM per device.

```python
import jax
import jax.numpy as jnp
from jax import lax

D = 3072
LAT_CH = 16
CH = 512
GROUPS = 32
IMAGES = 32
TOK = 4096
PACKED = 64
LAT_H = 128
LAT_W = 128


def rising_field(key, rise, noise):
    row_frac = jnp.arange(LAT_H, dtype=jnp.float32) / (LAT_H - 1)
    row_scale = jnp.exp(jnp.log(rise) * row_frac)[None, :, None, None]
    channel_key = jax.random.fold_in(key, 11)
    channel_mean = jax.random.uniform(channel_key, (IMAGES, 1, 1, LAT_CH), jnp.float32, -1.0, 1.0)
    return row_scale * (noise + channel_mean)


def draw_noisy_latent(key, part):
    key = jax.random.fold_in(key, 5)
    noise_key = jax.random.fold_in(key, 7)
    shape = (IMAGES, LAT_H, LAT_W, LAT_CH)
    noise = jnp.clip(jax.random.normal(noise_key, shape, jnp.float32), -5.0, 5.0)
    field = rising_field(key, 4.0, noise)
    return field.astype(jnp.bfloat16)


def shard_levels(key, extent, shards, low, top_value):
    level, own = 1.0, jax.random.fold_in(key, 6)
    for dim, blocks in shards:
        steps = jnp.exp(jax.random.uniform(jax.random.fold_in(own, dim), (blocks,), jnp.float32, low / len(shards), top_value / len(shards)))
        level = level * jnp.repeat(steps, extent[dim] // blocks).reshape([-1 if axis == dim else 1 for axis in range(len(extent))])
    return level


def scatter_about(own_key, shape, deviation, reach, shards=(), held_as=jnp.bfloat16):
    entries = jax.random.normal(own_key, shape, jnp.float32) * deviation
    if len(shards) > 0:
        entries = shard_levels(own_key, shape, shards, -0.22, 0.18) * entries
    return jnp.clip(entries, min=-reach, max=reach).astype(held_as)


def setup_inputs(seed: int = 0) -> dict:
    streams_of = jax.random.split(jax.random.key(seed), 14)
    return {
        "conditioning": scatter_about(streams_of[0], (IMAGES, D), 1.0, 6.0),
        "mod_weight": scatter_about(streams_of[1], (D, 2 * D), D ** -0.5, 0.109375, ((1, 512),)),
        "mod_bias": scatter_about(streams_of[2], (2 * D,), 3.0, 12.0, ((0, 512),), jnp.float32),
        "hidden": scatter_about(streams_of[3], (IMAGES, TOK, D), 1.0, 6.0, ((0, 8), (1, 64))),
        "proj_weight": scatter_about(streams_of[4], (D, PACKED), D ** -0.5, 0.109375),
        "proj_bias": scatter_about(streams_of[5], (PACKED,), 0.5, 3.0, (), jnp.float32),
        "noisy_latent": draw_noisy_latent(jax.random.fold_in(streams_of[13], 71), 0),
        "in_weight": scatter_about(streams_of[7], (9 * LAT_CH, CH), (9 * LAT_CH) ** -0.5, 0.5),
        "in_bias": scatter_about(streams_of[8], (CH,), 0.5, 3.0, (), jnp.float32),
        "norm_gain": jnp.clip(1.0 + 0.18 * jax.random.normal(streams_of[9], (CH,), jnp.float32), 0.1, 1.9),
        "norm_shift": scatter_about(streams_of[10], (CH,), 0.5, 3.0, (), jnp.float32),
        "conv_weight": scatter_about(streams_of[11], (9 * CH, CH), (9 * CH) ** -0.5, 0.09375, ((0, 64),)),
        "conv_bias": scatter_about(streams_of[12], (CH,), 0.5, 3.0, (), jnp.float32),
    }


def unfold_taps(padded, rows_out, cols_out):
    taps = [padded[row_shift:row_shift + rows_out, col_shift:col_shift + cols_out, :] for row_shift in range(3) for col_shift in range(3)]
    return jnp.concatenate(taps, axis=-1).reshape(rows_out * cols_out, -1)

def one_image(hidden_image, modulation_row, noisy_image, proj_weight, proj_bias, in_weight, in_bias, norm_gain, norm_shift, conv_weight, conv_bias):
    feature_dim = hidden_image.shape[1]
    scale_part = modulation_row[:feature_dim].astype(jnp.float32)
    shift_part = modulation_row[feature_dim:].astype(jnp.float32)
    values = hidden_image.astype(jnp.float32)
    centred = values - lax.optimization_barrier(jnp.mean(values, axis=-1, keepdims=True))
    variance = lax.optimization_barrier(jnp.mean(centred * centred, axis=-1, keepdims=True))
    modulated = (centred / jnp.sqrt(variance + 1e-06) * (1.0 + scale_part) + shift_part).astype(jnp.bfloat16)
    packed = jnp.dot(modulated, proj_weight, preferred_element_type=jnp.float32) + proj_bias
    lat_rows = LAT_H // 2
    lat_cols = LAT_W // 2
    velocity = packed.reshape(lat_rows, lat_cols, LAT_CH, 2, 2).transpose(0, 3, 1, 4, 2).reshape(LAT_H, LAT_W, LAT_CH)
    latent = ((noisy_image.astype(jnp.float32) - 0.75 * velocity) / 0.3611 + 0.1159).astype(jnp.bfloat16)
    padded = jnp.pad(latent, ((1, 1), (1, 1), (0, 0)))
    features = (jnp.dot(unfold_taps(padded, LAT_H, LAT_W), in_weight, preferred_element_type=jnp.float32) + in_bias).astype(jnp.bfloat16)
    grouped = features.astype(jnp.float32).reshape(LAT_H * LAT_W, GROUPS, CH // GROUPS)
    centre = lax.optimization_barrier(jnp.mean(grouped, axis=(0, 2), keepdims=True))
    spread = lax.optimization_barrier(jnp.mean((grouped - centre) ** 2, axis=(0, 2), keepdims=True))
    normed = ((grouped - centre) / jnp.sqrt(spread + 1e-06)).reshape(LAT_H * LAT_W, CH) * norm_gain + norm_shift
    activated = jax.nn.silu(normed).astype(jnp.bfloat16).reshape(LAT_H, LAT_W, CH)
    act_pad = jnp.pad(activated, ((1, 1), (1, 1), (0, 0)))
    branch = jnp.dot(unfold_taps(act_pad, LAT_H, LAT_W), conv_weight, preferred_element_type=jnp.float32)
    decoded = (branch + conv_bias).astype(jnp.bfloat16)
    return decoded.reshape(LAT_H, LAT_W, CH)

def reference(conditioning, mod_weight, mod_bias, hidden, proj_weight, proj_bias, noisy_latent, in_weight, in_bias, norm_gain, norm_shift, conv_weight, conv_bias):
    gated = jax.nn.silu(conditioning.astype(jnp.float32)).astype(jnp.bfloat16)
    modulation = (jnp.dot(gated, mod_weight, preferred_element_type=jnp.float32) + mod_bias).astype(jnp.bfloat16)

    def per_image(triple):
        return one_image(triple[0], triple[1], triple[2], proj_weight, proj_bias, in_weight, in_bias, norm_gain, norm_shift, conv_weight, conv_bias)
    return lax.map(per_image, (hidden, modulation, noisy_latent))
```

```python
import functools

import jax
import jax.numpy as jnp
import ml_dtypes
import numpy as np
from jax import lax
from jax.experimental import pallas as pl
from jax.experimental.pallas import tpu as pltpu
from jax.sharding import PartitionSpec as P

F32 = jnp.float32
BF16 = jnp.bfloat16
NT = (((1,), (1,)), ((), ()))
N_IMG = 4
COLS = 64
LANES = 128


def tables():
    taps = np.zeros((2, 2, 256, 144), np.float32)
    for odd in range(2):
        for low in range(2):
            for block in range(2):
                for down in range(2):
                    for k in range(16):
                        for i in range(2):
                            for j in range(2):
                                a = 2 * down + i - low
                                b = 2 * block + j + odd - 1
                                if 0 <= a <= 2 and 0 <= b <= 2:
                                    row = block * 128 + down * 64 + 4 * k + 2 * i + j
                                    taps[odd, low, row, (3 * a + b) * 16 + k] = 1
    split = np.zeros((128, 128), np.float32)
    for j in range(2):
        for c in range(64):
            split[j * 64 + c, 2 * c + j] = 1
    place = np.zeros((2, 4, 128, 128), np.float32)
    for j in range(2):
        for n in range(4):
            for i in range(2):
                for k in range(16):
                    for twin in range(2):
                        place[j, n, n * 32 + i * 16 + k, twin * 64 + 4 * k + 2 * i + j] = 1
    widen = np.zeros((512, 384), np.float32)
    for q in range(4):
        for l in range(96):
            widen[q * 128 + l, q * 96 + l] = 1
    channel = np.arange(512)
    same = (channel[:, None] // 16 == channel[None, :] // 16).astype(np.float32)
    spread = (np.arange(128)[:, None] % 32 == channel[None, :] // 16).astype(np.float32)
    kinds = (
        taps.reshape(1024, 144),
        split,
        place.reshape(1024, 128),
        widen,
        same,
        spread,
    )
    return [k.astype(ml_dtypes.bfloat16) for k in kinds]


def thirds(x):
    first = x.astype(BF16).astype(F32)
    rest = x - first
    second = rest.astype(BF16).astype(F32)
    third = rest - second
    return jnp.concatenate([first, second, third, jnp.zeros_like(x)], axis=0).astype(BF16)


def exact_dot(x, ones, dims):
    rows = x.shape[0]
    y = lax.dot_general(thirds(x), ones, dims, preferred_element_type=F32)
    return y[:rows] + y[rows : 2 * rows] + y[2 * rows : 3 * rows]


NN = (((1,), (0,)), ((), ()))


def kernel(
    nz,
    ngrp,
    cond_ref,
    modw_ref,
    modb_ref,
    hid_hbm,
    projw_ref,
    projb_ref,
    noisy_ref,
    inw_ref,
    inb_ref,
    gain_ref,
    shift_ref,
    convw_ref,
    convb_ref,
    taps_hbm,
    split_ref,
    place_ref,
    widen_ref,
    same_ref,
    spread_ref,
    out_ref,
    hid_ref,
    taps_ref,
    xn_ref,
    mod_ref,
    sc_ref,
    a1src,
    a1buf,
    a3buf,
    npk_ref,
    lat_ref,
    halo_ref,
    wb_ref,
    feat_ref,
    act_ref,
    c1buf,
    c2buf,
    stg_ref,
    rcv_ref,
    wbuf,
    ld_sem,
    sw_sem,
    a1_s,
    a1_r,
    a2_s,
    a2_r,
    a3_s,
    a3_r,
    b_s,
    b_r,
    c1_s,
    c1_r,
    c2_s,
    c2_r,
    zp_s,
    zp_r,
    zm_s,
    zm_r,
    y_s,
    y_r,
    k_s,
    k_r,
):
    nseq = 4 * nz
    s = lax.axis_index("seq")
    g = lax.axis_index("grp")
    z = lax.div(s, 4)
    q = lax.rem(s, 4)
    ylo = lax.div(q, 2)
    core = lax.rem(q, 2)
    x = lax.div(g, 2)
    yhi = lax.rem(g, 2)
    yy = 2 * yhi + ylo

    def at_z(zz):
        return {"seq": zz * 4 + q, "grp": g}

    def at_y(step):
        new = lax.rem(yy + 4 + step, 4)
        return {
            "seq": z * 4 + lax.rem(new, 2) * 2 + core,
            "grp": x * 2 + lax.div(new, 2),
        }

    def at_q(o):
        return {"seq": z * 4 + lax.rem(q + o, 4), "grp": g}

    def at_g(o):
        return {"seq": s, "grp": lax.rem(g + o, ngrp)}

    def at_s(step):
        return {"seq": lax.rem(s + nseq + step, nseq), "grp": g}

    mate = {"seq": z * 4 + ylo * 2 + (1 - core), "grp": g}

    def zmod(o):
        return lax.rem(z + nz + o, nz)

    pending = []

    def send(src, dst, ssem, rsem, where):
        copy = pltpu.make_async_remote_copy(
            src_ref=src,
            dst_ref=dst,
            send_sem=ssem,
            recv_sem=rsem,
            device_id=where,
            device_id_type=pl.DeviceIdType.MESH,
        )
        copy.start()
        pending.append(copy)
        return copy

    load_hid = pltpu.make_async_copy(hid_hbm, hid_ref, ld_sem.at[0])
    load_hid.start()
    load_taps = pltpu.make_async_copy(taps_hbm, taps_ref, ld_sem.at[1])
    load_taps.start()

    barrier = pltpu.get_barrier_semaphore()
    greeted = (
        [at_z(zmod(o)) for o in range(1, nz)]
        + [at_g(o) for o in range(1, ngrp)]
        + [at_q(o) for o in range(1, 4)]
        + [at_y(1), at_y(-1), at_s(1), at_s(-1), mate]
    )
    for where in greeted:
        pl.semaphore_signal(barrier, inc=1, device_id=where, device_id_type=pl.DeviceIdType.MESH)

    rows = convw_ref.shape[0]
    whole = convw_ref[...].astype(F32)
    stg_ref[0] = whole[:, :256]
    stg_ref[1] = whole[:, 256:]
    v = cond_ref[...].astype(F32)
    gated = (v / (1.0 + jnp.exp(-v))).astype(BF16)
    own_mod = lax.dot_general(gated, modw_ref[...], NT, preferred_element_type=F32) + modb_ref[...]
    mcols = own_mod.shape[1]
    spot = lax.broadcasted_iota(jnp.int32, (mcols, LANES), 0) + g * mcols
    lane = lax.broadcasted_iota(jnp.int32, (mcols, LANES), 1)
    put = jnp.where(spot == lane, 1.0, 0.0).astype(BF16)
    placed = jnp.dot(own_mod.astype(BF16), put, preferred_element_type=F32)
    for o in range(ngrp):
        a1src[o] = placed[N_IMG * o : N_IMG * (o + 1)]

    pl.semaphore_wait(barrier, len(greeted))

    swap = send(stg_ref.at[1 - core], rcv_ref, sw_sem.at[0], sw_sem.at[1], mate)
    a1 = []
    for o in range(1, ngrp):
        peer = at_g(o)
        a1.append(
            send(a1src.at[peer["grp"]], a1buf.at[o], a1_s.at[o - 1], a1_r.at[o - 1], peer)
        )

    def chunk(zz, half_y):
        return pl.ds(pl.multiple_of((2 * zz + half_y) * (2 * rows), 16), 2 * rows)

    swap.wait_recv()
    here = stg_ref[core]
    there = rcv_ref[...]
    top = jnp.where(core == 0, here, there)
    bottom = jnp.where(core == 0, there, here)
    wbuf[core, chunk(z, ylo), :] = jnp.concatenate([top, bottom], axis=0).astype(BF16)

    n_plus, n_minus = nz // 2, nz // 2 - 1
    zp, zm, ycopies, kcopies = {}, {}, {}, []

    def spread_chunk(slot, zz):
        at = chunk(zz, ylo)
        ycopies[slot] = [
            send(
                wbuf.at[core, at, pl.ds(0, 128)],
                wbuf.at[core, at, pl.ds(0, 128)],
                y_s.at[slot, 0],
                y_r.at[slot, 0],
                at_y(1),
            ),
            send(
                wbuf.at[core, at, pl.ds(128, 128)],
                wbuf.at[core, at, pl.ds(128, 128)],
                y_s.at[slot, 1],
                y_r.at[slot, 1],
                at_y(-1),
            ),
        ]
        kcopies.append(
            send(wbuf.at[core, at], wbuf.at[core, at], k_s.at[slot, 0], k_r.at[slot, 0], mate)
        )

    def pass_y(slot, zz):
        for copy in ycopies[slot]:
            copy.wait_recv()
        at = chunk(zz, 1 - ylo)
        kcopies.append(
            send(wbuf.at[core, at], wbuf.at[core, at], k_s.at[slot, 1], k_r.at[slot, 1], mate)
        )

    def slots(k):
        if k == 0:
            return [(0, zmod(0))]
        out = []
        if k <= n_plus:
            out.append((2 * k - 1, zmod(-k)))
        if k <= n_minus:
            out.append((2 * k, zmod(k)))
        return out

    def tick(k):
        if 1 <= k <= n_plus:
            zp[k].wait_recv()
        if k < n_plus:
            at = chunk(zmod(-k), ylo)
            zp[k + 1] = send(
                wbuf.at[core, at], wbuf.at[core, at], zp_s.at[k], zp_r.at[k], at_z(zmod(1))
            )
        if 1 <= k <= n_minus:
            zm[k].wait_recv()
        if k < n_minus:
            at = chunk(zmod(k), ylo)
            zm[k + 1] = send(
                wbuf.at[core, at], wbuf.at[core, at], zm_s.at[k], zm_r.at[k], at_z(zmod(-1))
            )
        if k <= n_plus:
            for slot, zz in slots(k):
                spread_chunk(slot, zz)
        if 1 <= k <= n_plus + 1:
            for slot, zz in slots(k - 1):
                pass_y(slot, zz)

    last_tick = n_plus + 1
    clock = [0]

    def next_tick():
        if clock[0] <= last_tick:
            tick(clock[0])
            clock[0] += 1

    next_tick()

    for copy in a1:
        copy.wait_recv()
    merged = a1src[g]
    for o in range(1, ngrp):
        merged = merged + a1buf[o]
    a3buf[q, z] = merged
    a2 = []
    for o in range(1, nz):
        a2.append(
            send(a3buf.at[q, z], a3buf.at[q, z], a2_s.at[o - 1], a2_r.at[o - 1], at_z(zmod(o)))
        )

    load_hid.wait()

    def norm_rows(first, count):
        def body(step, carry):
            at = pl.ds(pl.multiple_of(step * 16, 16), 16)
            h = hid_ref[at, :].astype(F32)
            c = h - jnp.mean(h, axis=-1, keepdims=True)
            var = jnp.mean(c * c, axis=-1, keepdims=True)
            xn_ref[at, :] = c * lax.rsqrt(var + 1e-06)
            return carry

        lax.fori_loop(first, first + count, body, 0)

    norm_rows(0, 8)
    next_tick()
    for copy in a2:
        copy.wait_recv()
    a3 = []
    for o in range(1, 4):
        a3.append(send(a3buf.at[q], a3buf.at[q], a3_s.at[o - 1], a3_r.at[o - 1], at_q(o)))
    norm_rows(8, 8)

    de = lax.dot_general(split_ref[...], noisy_ref[...], NT, preferred_element_type=F32).astype(BF16)
    for n in range(N_IMG):
        npk_ref[pl.ds(n * COLS, COLS), :] = jnp.dot(
            de[:64], place_ref[pl.ds(n * 128, 128), :], preferred_element_type=F32
        ) + jnp.dot(de[64:], place_ref[pl.ds(512 + n * 128, 128), :], preferred_element_type=F32)
    next_tick()
    load_taps.wait()
    for odd in range(2):
        for low in range(2):
            wb_ref[odd, :, pl.ds(512 * low, 512)] = jnp.dot(
                taps_ref[pl.ds((2 * odd + low) * 256, 256), :],
                inw_ref[...],
                preferred_element_type=F32,
            ).astype(BF16)

    for copy in a3:
        copy.wait_recv()
    for qq in range(4):
        for zz in range(nz):
            sc_ref[pl.ds(N_IMG * zz, N_IMG), pl.ds(LANES * qq, LANES)] = a3buf[qq, zz]
    table = jnp.dot(sc_ref[...].astype(BF16), widen_ref[...], preferred_element_type=F32)
    half = nz // 2
    for n in range(N_IMG):
        for zz in range(half):
            at = (pl.ds(n * COLS, COLS), pl.ds(384 * zz, 384))
            lift = table[N_IMG * zz + n : N_IMG * zz + n + 1]
            move = table[N_IMG * (zz + half) + n : N_IMG * (zz + half) + n + 1]
            mod_ref[at] = (xn_ref[at] * (1.0 + lift) + move).astype(BF16)
    proj = projw_ref[...]
    packed = lax.dot_general(
        mod_ref[...], jnp.concatenate([proj, proj], axis=0), NT, preferred_element_type=F32
    )
    packed = packed + projb_ref[...]
    lat_ref[...] = ((npk_ref[...] - 0.75 * packed) / 0.3611 + 0.1159).astype(BF16)
    down = send(lat_ref, halo_ref.at[0], b_s.at[0], b_r.at[0], at_s(1))
    up = send(lat_ref, halo_ref.at[1], b_s.at[1], b_r.at[1], at_s(-1))
    next_tick()

    down.wait_recv()
    up.wait_recv()
    lat = lat_ref[...].astype(F32)
    above = jnp.where(s == 0, 0.0, halo_ref[0].astype(F32))
    below = jnp.where(s == nseq - 1, 0.0, halo_ref[1].astype(F32))
    left = lax.broadcasted_iota(jnp.int32, (N_IMG * COLS, LANES), 1) < 64
    column = lax.rem(lax.broadcasted_iota(jnp.int32, (N_IMG * COLS, LANES), 0), COLS)
    for pair in range(2):
        both = jnp.where(left, above, lat) if pair == 0 else jnp.where(left, lat, below)
        before = jnp.where(column == 0, 0.0, pltpu.roll(both, 1, 0))
        after = jnp.where(column == COLS - 1, 0.0, pltpu.roll(both, N_IMG * COLS - 1, 0))
        for odd in range(2):
            parts = [before, both] if odd == 0 else [both, after]
            patch = jnp.concatenate(parts, axis=1).astype(BF16)
            for low in range(2):
                feat_ref[2 * pair + low, odd] = (
                    jnp.dot(
                        patch, wb_ref[odd, :, pl.ds(512 * low, 512)], preferred_element_type=F32
                    )
                    + inb_ref[...]
                ).astype(BF16)
    next_tick()

    own = [(1, 0), (1, 1), (2, 0), (2, 1)]
    means, moments = [], []
    for n in range(N_IMG):
        at = pl.ds(n * COLS, COLS)
        total = jnp.zeros((1, 512), F32)
        for h, odd in own:
            total = total + jnp.sum(feat_ref[h, odd, at, :].astype(F32), axis=0, keepdims=True)
        mean = total / 256.0
        moment = jnp.zeros((1, 512), F32)
        for h, odd in own:
            d = feat_ref[h, odd, at, :].astype(F32) - mean
            moment = moment + jnp.sum(d * d, axis=0, keepdims=True)
        means.append(mean)
        moments.append(moment)
    empty = jnp.zeros((4, 512), F32)
    mean4 = jnp.concatenate(means + [empty], axis=0)
    moment4 = jnp.concatenate(moments + [empty], axis=0)
    group = exact_dot(mean4, same_ref[...], NN) / 16.0
    gap = mean4 - group
    moment4 = moment4 + 256.0 * gap * gap
    packed8 = exact_dot(
        jnp.concatenate([mean4[:4], moment4[:4]], axis=0), spread_ref[...], NT
    )
    row8 = lax.broadcasted_iota(jnp.int32, (8, LANES), 0)
    lane8 = lax.broadcasted_iota(jnp.int32, (8, LANES), 1)
    mine = lax.rem(row8, 4) == lax.div(lane8, 32)
    packed8 = jnp.where(mine, packed8, 0.0)
    c1buf[q, 0:1] = jnp.sum(packed8[:4], axis=0, keepdims=True) / 16.0
    c1buf[q, 1:2] = jnp.sum(packed8[4:], axis=0, keepdims=True)
    c1 = []
    for o in range(1, 4):
        c1.append(send(c1buf.at[q], c1buf.at[q], c1_s.at[o - 1], c1_r.at[o - 1], at_q(o)))
    next_tick()
    for copy in c1:
        copy.wait_recv()

    def merge(buf, count, each):
        centre = buf[0, 0:1]
        for o in range(1, count):
            centre = centre + buf[o, 0:1]
        centre = centre / count
        square = jnp.zeros_like(centre)
        for o in range(count):
            d = buf[o, 0:1] - centre
            square = square + buf[o, 1:2] + each * (d * d)
        return centre, square

    centre, square = merge(c1buf, 4, 4096.0)
    c2buf[z, 0:1] = centre
    c2buf[z, 1:2] = square
    c2 = []
    for o in range(1, nz):
        c2.append(
            send(c2buf.at[z], c2buf.at[z], c2_s.at[o - 1], c2_r.at[o - 1], at_z(zmod(o)))
        )
    next_tick()
    for copy in c2:
        copy.wait_recv()
    centre, square = merge(c2buf, nz, 4.0 * 4096.0)
    rate = lax.rsqrt(square / (4096.0 * nseq) + 1e-06)
    both8 = jnp.where(mine, jnp.where(row8 < 4, centre, rate), 0.0)
    wide = exact_dot(both8, spread_ref[...], NN)

    next_tick()
    first_row = lax.broadcasted_iota(jnp.int32, (COLS, 512), 0)
    keep_top = jnp.where(s == 0, 0.0, 1.0)
    keep_bottom = jnp.where(s == nseq - 1, 0.0, 1.0)
    for n in range(N_IMG):
        at = pl.ds(n * COLS, COLS)
        cen = wide[n : n + 1]
        slope = wide[4 + n : 5 + n] * gain_ref[...]
        for h in range(4):
            for odd in range(2):
                t = (feat_ref[h, odd, at, :].astype(F32) - cen) * slope + shift_ref[...]
                t = 0.5 * t
                act = t + t * jnp.tanh(t)
                if h == 0:
                    act = act * keep_top
                if h == 3:
                    act = act * keep_bottom
                act_ref[h, 1 + odd, at, :] = act.astype(BF16)
                if odd == 0:
                    moved = jnp.where(first_row == COLS - 1, 0.0, pltpu.roll(act, COLS - 1, 0))
                    act_ref[h, 3, at, :] = moved.astype(BF16)
                else:
                    moved = jnp.where(first_row == 0, 0.0, pltpu.roll(act, 1, 0))
                    act_ref[h, 0, at, :] = moved.astype(BF16)
    while clock[0] <= last_tick:
        next_tick()
    for copy in kcopies:
        copy.wait_recv()

    for rho in range(2):
        for part in range(2):
            acc = None
            for a in range(3):
                for b in range(3):
                    lhs = act_ref[rho + a, pl.ds(b, 2)].reshape(2 * N_IMG * COLS, 512)
                    term = jnp.dot(
                        lhs,
                        wbuf[part, pl.ds((3 * a + b) * 512, 512), :],
                        preferred_element_type=F32,
                    )
                    acc = term if acc is None else acc + term
            acc = (acc + convb_ref[:, pl.ds(256 * part, 256)]).astype(BF16)
            for odd in range(2):
                for n in range(N_IMG):
                    first = (odd * N_IMG + n) * COLS
                    out_ref[n, rho, :, pl.ds(512 * odd + 256 * part, 256)] = acc[
                        first : first + COLS
                    ]
    for copy in pending:
        copy.wait_send()


def on_device(
    nz,
    ngrp,
    conditioning,
    mod_weight,
    mod_bias,
    hidden,
    proj_weight,
    proj_bias,
    noisy_latent,
    in_weight,
    in_bias,
    norm_gain,
    norm_shift,
    conv_weight,
    conv_bias,
):
    width = hidden.shape[2]
    tokens = N_IMG * COLS
    shard = conv_weight.shape[0]
    vmem = pl.BlockSpec(memory_space=pltpu.VMEM)
    hbm = pl.BlockSpec(memory_space=pl.ANY)
    dma = pltpu.SemaphoreType.DMA
    n_plus = nz // 2
    consts = [jnp.asarray(t) for t in tables()]
    scratch = [
        pltpu.VMEM((tokens, width), BF16),
        pltpu.VMEM((1024, 144), BF16),
        pltpu.VMEM((tokens, width), F32),
        pltpu.VMEM((tokens, width), BF16),
        pltpu.VMEM((N_IMG * nz, 512), F32),
        pltpu.VMEM((ngrp, N_IMG, LANES), F32),
        pltpu.VMEM((ngrp, N_IMG, LANES), F32),
        pltpu.VMEM((4, nz, N_IMG, LANES), F32),
        pltpu.VMEM((tokens, LANES), F32),
        pltpu.VMEM((tokens, LANES), BF16),
        pltpu.VMEM((2, tokens, LANES), BF16),
        pltpu.VMEM((2, 256, 1024), BF16),
        pltpu.VMEM((4, 2, tokens, 512), BF16),
        pltpu.VMEM((4, 4, tokens, 512), BF16),
        pltpu.VMEM((4, 2, LANES), F32),
        pltpu.VMEM((nz, 2, LANES), F32),
        pltpu.VMEM((2, shard, 256), F32),
        pltpu.VMEM((shard, 256), F32),
        pltpu.VMEM((2, shard * 4 * nz, 256), BF16),
        dma((2,)),
        dma((2,)),
        dma((ngrp - 1,)),
        dma((ngrp - 1,)),
        dma((nz - 1,)),
        dma((nz - 1,)),
        dma((3,)),
        dma((3,)),
        dma((2,)),
        dma((2,)),
        dma((3,)),
        dma((3,)),
        dma((nz - 1,)),
        dma((nz - 1,)),
        dma((n_plus,)),
        dma((n_plus,)),
        dma((n_plus,)),
        dma((n_plus,)),
        dma((nz, 2)),
        dma((nz, 2)),
        dma((nz, 2)),
        dma((nz, 2)),
    ]
    out = pl.pallas_call(
        functools.partial(kernel, nz, ngrp),
        out_shape=jax.ShapeDtypeStruct((N_IMG, 2, COLS, 1024), BF16),
        in_specs=[vmem] * 3 + [hbm] + [vmem] * 9 + [hbm] + [vmem] * 5,
        out_specs=vmem,
        scratch_shapes=scratch,
        compiler_params=pltpu.CompilerParams(
            collective_id=0, has_side_effects=True, vmem_limit_bytes=56 * 1024 * 1024
        ),
    )(
        conditioning,
        mod_weight.T,
        mod_bias.reshape(1, -1),
        hidden.reshape(tokens, width),
        proj_weight.T,
        jnp.concatenate([proj_bias, proj_bias]).reshape(1, -1),
        noisy_latent.transpose(0, 1, 3, 2).reshape(128, 128),
        in_weight,
        in_bias.reshape(1, -1),
        norm_gain.reshape(1, -1),
        norm_shift.reshape(1, -1),
        conv_weight,
        conv_bias.reshape(1, -1),
        *consts,
    )
    return out.reshape(N_IMG, 2, 2 * COLS, 512)


def solution(mesh):
    nz = mesh.shape["seq"] // 4
    ngrp = mesh.shape["grp"]
    placed = (
        P(),
        P(None, ("seq", "grp")),
        P(("seq", "grp")),
        P("grp", "seq", None),
        P(),
        P(),
        P("grp", "seq", None, None),
        P(),
        P(),
        P(),
        P(),
        P("seq", None),
        P(),
    )
    return jax.shard_map(
        functools.partial(on_device, nz, ngrp),
        mesh=mesh,
        in_specs=placed,
        out_specs=P("grp", "seq", None, None),
        check_vma=False,
    )
```

```python
import functools

import jax
import jax.numpy as jnp
import ml_dtypes
import numpy as np
from jax import lax
from jax.experimental import pallas as pl
from jax.experimental.pallas import tpu as pltpu
from jax.sharding import PartitionSpec as P

F32 = jnp.float32
BF16 = jnp.bfloat16
NT = (((1,), (1,)), ((), ()))
N_IMG = 4
COLS = 64
LANES = 128


def tables():
    taps = np.zeros((2, 2, 256, 144), np.float32)
    for odd in range(2):
        for low in range(2):
            for block in range(2):
                for down in range(2):
                    for k in range(16):
                        for i in range(2):
                            for j in range(2):
                                a = 2 * down + i - low
                                b = 2 * block + j + odd - 1
                                if 0 <= a <= 2 and 0 <= b <= 2:
                                    row = block * 128 + down * 64 + 4 * k + 2 * i + j
                                    taps[odd, low, row, (3 * a + b) * 16 + k] = 1
    split = np.zeros((128, 128), np.float32)
    for j in range(2):
        for c in range(64):
            split[j * 64 + c, 2 * c + j] = 1
    place = np.zeros((2, 4, 128, 128), np.float32)
    for j in range(2):
        for n in range(4):
            for i in range(2):
                for k in range(16):
                    for twin in range(2):
                        place[j, n, n * 32 + i * 16 + k, twin * 64 + 4 * k + 2 * i + j] = 1
    widen = np.zeros((512, 384), np.float32)
    for q in range(4):
        for l in range(96):
            widen[q * 128 + l, q * 96 + l] = 1
    channel = np.arange(512)
    same = (channel[:, None] // 16 == channel[None, :] // 16).astype(np.float32)
    spread = (np.arange(128)[:, None] % 32 == channel[None, :] // 16).astype(np.float32)
    kinds = (
        taps.reshape(1024, 144),
        split,
        place.reshape(1024, 128),
        widen,
        same,
        spread,
    )
    return [k.astype(ml_dtypes.bfloat16) for k in kinds]


def thirds(x):
    first = x.astype(BF16).astype(F32)
    rest = x - first
    second = rest.astype(BF16).astype(F32)
    third = rest - second
    return jnp.concatenate([first, second, third, jnp.zeros_like(x)], axis=0).astype(BF16)


def exact_dot(x, ones, dims):
    rows = x.shape[0]
    y = lax.dot_general(thirds(x), ones, dims, preferred_element_type=F32)
    return y[:rows] + y[rows : 2 * rows] + y[2 * rows : 3 * rows]


NN = (((1,), (0,)), ((), ()))


def kernel(
    nz,
    ngrp,
    cond_hbm,
    modw_hbm,
    modb_ref,
    hid_hbm,
    projw_hbm,
    projb_ref,
    noisy_hbm,
    inw_hbm,
    inb_ref,
    gain_ref,
    shift_ref,
    convw_hbm,
    convb_ref,
    taps_hbm,
    split_hbm,
    place_hbm,
    widen_hbm,
    same_hbm,
    spread_hbm,
    out_ref,
    cond_ref,
    modw_ref,
    hid_ref,
    projw_ref,
    noisy_ref,
    inw_ref,
    convw_ref,
    taps_ref,
    split_ref,
    place_ref,
    widen_ref,
    same_ref,
    spread_ref,
    xn_ref,
    mod_ref,
    sc_ref,
    a1src,
    a1buf,
    a2buf,
    npk_ref,
    lat_ref,
    halo_ref,
    wb_ref,
    feat_ref,
    act_ref,
    c1buf,
    c2buf,
    stg_ref,
    rcv_ref,
    wbuf,
    ld_sem,
    sw_sem,
    a1_s,
    a1_r,
    a2_s,
    a2_r,
    b_s,
    b_r,
    c1_s,
    c1_r,
    c2_s,
    c2_r,
    z_s,
    z_r,
    x_s,
    x_r,
    y_s,
    y_r,
    k_s,
    k_r,
):
    nseq = 4 * nz
    s = lax.axis_index("seq")
    g = lax.axis_index("grp")
    z = lax.div(s, 4)
    q = lax.rem(s, 4)
    ylo = lax.div(q, 2)
    core = lax.rem(q, 2)
    x = lax.div(g, 2)
    yhi = lax.rem(g, 2)
    yy = 2 * yhi + ylo

    def at_z(zz):
        return {"seq": zz * 4 + q, "grp": g}

    def at_y(step):
        new = lax.rem(yy + 4 + step, 4)
        return {
            "seq": z * 4 + lax.rem(new, 2) * 2 + core,
            "grp": x * 2 + lax.div(new, 2),
        }

    def at_q(o):
        return {"seq": z * 4 + lax.rem(q + o, 4), "grp": g}

    def at_g(o):
        return {"seq": s, "grp": lax.rem(g + o, ngrp)}

    def at_s(step):
        return {"seq": lax.rem(s + nseq + step, nseq), "grp": g}

    mate = {"seq": z * 4 + ylo * 2 + (1 - core), "grp": g}

    def zmod(o):
        return lax.rem(z + nz + o, nz)

    pending = []

    def send(src, dst, ssem, rsem, where):
        copy = pltpu.make_async_remote_copy(
            src_ref=src,
            dst_ref=dst,
            send_sem=ssem,
            recv_sem=rsem,
            device_id=where,
            device_id_type=pl.DeviceIdType.MESH,
        )
        copy.start()
        pending.append(copy)
        return copy

    def at_x(m):
        return {"seq": s, "grp": lax.rem(x + m, ngrp // 2) * 2 + yhi}

    def at_plane(oq, og):
        return {"seq": z * 4 + lax.rem(q + oq, 4), "grp": lax.rem(g + og, ngrp)}

    plane = [(oq, og) for oq in range(4) for og in range(ngrp) if oq or og]
    barrier = pltpu.get_barrier_semaphore()
    greeted = (
        [at_z(zmod(o)) for o in sorted(range(1, nz), key=lambda o: -min(o, nz - o))]
        + [at_plane(oq, og) for oq, og in plane]
        + [at_s(1), at_s(-1)]
    )
    for where in greeted:
        pl.semaphore_signal(barrier, inc=1, device_id=where, device_id_type=pl.DeviceIdType.MESH)

    loads = []
    for i, (src, dst) in enumerate(
        (
            (convw_hbm, convw_ref),
            (cond_hbm, cond_ref),
            (modw_hbm, modw_ref),
            (hid_hbm, hid_ref),
            (noisy_hbm, noisy_ref),
            (split_hbm, split_ref),
            (place_hbm, place_ref),
            (inw_hbm, inw_ref),
            (taps_hbm, taps_ref),
            (projw_hbm, projw_ref),
            (widen_hbm, widen_ref),
            (same_hbm, same_ref),
            (spread_hbm, spread_ref),
        )
    ):
        loads.append(pltpu.make_async_copy(src, dst, ld_sem.at[i]))
        loads[-1].start()

    for copy in loads[:3]:
        copy.wait()
    rows = convw_ref.shape[0]
    whole = convw_ref[...].astype(F32)
    stg_ref[0] = whole[:, :256]
    stg_ref[1] = whole[:, 256:]
    v = cond_ref[...].astype(F32)
    gated = (v / (1.0 + jnp.exp(-v))).astype(BF16)
    own_mod = lax.dot_general(gated, modw_ref[...], NT, preferred_element_type=F32) + modb_ref[...]
    mcols = own_mod.shape[1]
    spot = lax.broadcasted_iota(jnp.int32, (mcols, LANES), 0) + g * mcols
    lane = lax.broadcasted_iota(jnp.int32, (mcols, LANES), 1)
    put = jnp.where(spot == lane, 1.0, 0.0).astype(BF16)
    placed = jnp.dot(own_mod.astype(BF16), put, preferred_element_type=F32)
    for o in range(ngrp):
        a1src[o] = placed[N_IMG * o : N_IMG * (o + 1)]

    pl.semaphore_wait(barrier, len(greeted))

    swap = send(stg_ref.at[1 - core], rcv_ref, sw_sem.at[0], sw_sem.at[1], mate)
    a1 = []
    for i, (oq, og) in enumerate(plane):
        peer = at_plane(oq, og)
        a1.append(send(a1src.at[peer["grp"]], a1buf.at[q, og], a1_s.at[i], a1_r.at[i], peer))

    def chunk(zz, half_y):
        return pl.ds(pl.multiple_of((2 * zz + half_y) * (2 * rows), 16), 2 * rows)

    swap.wait_recv()
    here = stg_ref[core]
    there = rcv_ref[...]
    top = jnp.where(core == 0, here, there)
    bottom = jnp.where(core == 0, there, here)
    wbuf[core, chunk(z, ylo), :] = jnp.concatenate([top, bottom], axis=0).astype(BF16)

    nx = ngrp // 2

    def wanted(j, xx):
        if nx == 1:
            return j
        quarter = nz // 4
        near = [xx, nz // 2 - xx, nz // 2 + xx, nz - xx][j]
        return jnp.where(xx == 0, quarter * j, near)

    def guarded(j, xx, act):
        if j == 0:
            pl.when(xx > 0)(act)
        else:
            act()

    per = nz if nx == 1 else 4
    first, second = ([1], [0]) if nx == 1 else ([0, 3], [1, 2])

    def copy_of(src, dst, ssem, rsem, where):
        return pltpu.make_async_remote_copy(
            src_ref=src,
            dst_ref=dst,
            send_sem=ssem,
            recv_sem=rsem,
            device_id=where,
            device_id_type=pl.DeviceIdType.MESH,
        )

    def z_copy(j):
        at = wbuf.at[core, chunk(z, ylo)]
        return copy_of(at, at, z_s.at[j], z_r.at[j], at_z(lax.rem(z + nz - wanted(j, x), nz)))

    def x_copy(m, j):
        at = wbuf.at[core, chunk(lax.rem(z + wanted(j, x), nz), ylo)]
        return copy_of(at, at, x_s.at[m, j], x_r.at[m, j], at_x(m))

    def zz_of(m, j):
        return lax.rem(z + wanted(j, lax.rem(x + nx - m, nx)), nz)

    def y_copies(slot, zz):
        at = wbuf.at[core, chunk(zz, ylo)]
        return [
            copy_of(
                at.at[:, pl.ds(128 * i, 128)],
                at.at[:, pl.ds(128 * i, 128)],
                y_s.at[slot, i],
                y_r.at[slot, i],
                at_y(1 - 2 * i),
            )
            for i in range(2)
        ]

    def k_copy(slot, zz, other):
        at = wbuf.at[core, chunk(zz, 1 - ylo if other else ylo)]
        return copy_of(at, at, k_s.at[slot, other], k_r.at[slot, other], mate)

    own_slot = nx * per
    every = [(m, j) for m in range(nx) for j in range(per)]

    def origin(m):
        return lax.rem(x + nx - m, nx)

    def start_own():
        for j in range(per):
            guarded(j, x, lambda j=j: z_copy(j).start())
        for copy in y_copies(own_slot, z):
            copy.start()
        k_copy(own_slot, z, 0).start()

    def onward(m, j):
        for copy in y_copies(m * per + j, zz_of(m, j)):
            copy.start()
        k_copy(m * per + j, zz_of(m, j), 0).start()

    def take_z(js):
        for j in js:

            def act(j=j):
                z_copy(j).wait_recv()
                for m in range(1, nx):
                    x_copy(m, j).start()
                onward(0, j)

            guarded(j, x, act)

    def take_x(js):
        for m in range(1, nx):
            for j in js:

                def act(m=m, j=j):
                    x_copy(m, j).wait_recv()
                    onward(m, j)

                guarded(j, origin(m), act)

    def take_y_slot(slot, zz):
        for copy in y_copies(slot, zz):
            copy.wait_recv()
        k_copy(slot, zz, 1).start()

    def take_y(js):
        for m in range(nx):
            for j in js:
                guarded(j, origin(m), lambda m=m, j=j: take_y_slot(m * per + j, zz_of(m, j)))

    def finish_gather():
        for other in range(2):
            k_copy(own_slot, z, other).wait_recv()
            for m, j in every:
                guarded(
                    j,
                    origin(m),
                    lambda m=m, j=j: k_copy(m * per + j, zz_of(m, j), other).wait_recv(),
                )

    def drain():
        for j in range(per):

            def sent(j=j):
                z_copy(j).wait_send()
                for m in range(1, nx):
                    x_copy(m, j).wait_send()

            guarded(j, x, sent)
        for copy in y_copies(own_slot, z):
            copy.wait_send()
        for other in range(2):
            k_copy(own_slot, z, other).wait_send()
        for m, j in every:

            def sent(m=m, j=j):
                for copy in y_copies(m * per + j, zz_of(m, j)):
                    copy.wait_send()
                for other in range(2):
                    k_copy(m * per + j, zz_of(m, j), other).wait_send()

            guarded(j, origin(m), sent)

    start_own()

    for copy in a1:
        copy.wait_recv()
    pieces = []
    for qq in range(4):
        piece = jnp.where(q == qq, a1src[g], jnp.zeros((N_IMG, LANES), F32))
        for og in range(ngrp):
            block = a1buf[qq, og]
            if og == 0:
                block = jnp.where(q == qq, 0.0, block)
            piece = piece + block
        pieces.append(piece)
    a2buf[z] = jnp.concatenate(pieces, axis=0).astype(BF16)
    a2 = []
    for o in sorted(range(1, nz), key=lambda o: -min(o, nz - o)):
        a2.append(
            send(a2buf.at[z], a2buf.at[z], a2_s.at[o - 1], a2_r.at[o - 1], at_z(zmod(o)))
        )

    take_z(first)
    for copy in loads[3:]:
        copy.wait()

    def norm_rows(first, count):
        def body(step, carry):
            at = pl.ds(pl.multiple_of(step * 16, 16), 16)
            h = hid_ref[at, :].astype(F32)
            c = h - jnp.mean(h, axis=-1, keepdims=True)
            var = jnp.mean(c * c, axis=-1, keepdims=True)
            xn_ref[at, :] = c * lax.rsqrt(var + 1e-06)
            return carry

        lax.fori_loop(first, first + count, body, 0)

    norm_rows(0, 8)
    take_x(first)
    norm_rows(8, 8)

    de = lax.dot_general(split_ref[...], noisy_ref[...], NT, preferred_element_type=F32).astype(BF16)
    for n in range(N_IMG):
        npk_ref[pl.ds(n * COLS, COLS), :] = jnp.dot(
            de[:64], place_ref[pl.ds(n * 128, 128), :], preferred_element_type=F32
        ) + jnp.dot(de[64:], place_ref[pl.ds(512 + n * 128, 128), :], preferred_element_type=F32)
    for odd in range(2):
        for low in range(2):
            wb_ref[odd, :, pl.ds(512 * low, 512)] = jnp.dot(
                taps_ref[pl.ds((2 * odd + low) * 256, 256), :],
                inw_ref[...],
                preferred_element_type=F32,
            ).astype(BF16)

    for copy in a2:
        copy.wait_recv()
    for zz in range(nz):
        block = a2buf[zz].astype(F32)
        for qq in range(4):
            sc_ref[pl.ds(N_IMG * zz, N_IMG), pl.ds(LANES * qq, LANES)] = block[
                N_IMG * qq : N_IMG * (qq + 1)
            ]
    table = jnp.dot(sc_ref[...].astype(BF16), widen_ref[...], preferred_element_type=F32)
    half = nz // 2
    for n in range(N_IMG):
        for zz in range(half):
            at = (pl.ds(n * COLS, COLS), pl.ds(384 * zz, 384))
            lift = table[N_IMG * zz + n : N_IMG * zz + n + 1]
            move = table[N_IMG * (zz + half) + n : N_IMG * (zz + half) + n + 1]
            mod_ref[at] = (xn_ref[at] * (1.0 + lift) + move).astype(BF16)
    proj = projw_ref[...]
    packed = lax.dot_general(
        mod_ref[...], jnp.concatenate([proj, proj], axis=0), NT, preferred_element_type=F32
    )
    packed = packed + jnp.concatenate([projb_ref[...], projb_ref[...]], axis=1)
    lat_ref[...] = ((npk_ref[...] - 0.75 * packed) / 0.3611 + 0.1159).astype(BF16)
    down = send(lat_ref, halo_ref.at[0], b_s.at[0], b_r.at[0], at_s(1))
    up = send(lat_ref, halo_ref.at[1], b_s.at[1], b_r.at[1], at_s(-1))
    take_z(second)
    take_y_slot(own_slot, z)

    down.wait_recv()
    up.wait_recv()
    lat = lat_ref[...].astype(F32)
    above = jnp.where(s == 0, 0.0, halo_ref[0].astype(F32))
    below = jnp.where(s == nseq - 1, 0.0, halo_ref[1].astype(F32))
    left = lax.broadcasted_iota(jnp.int32, (N_IMG * COLS, LANES), 1) < 64
    column = lax.rem(lax.broadcasted_iota(jnp.int32, (N_IMG * COLS, LANES), 0), COLS)
    for pair in range(2):
        both = jnp.where(left, above, lat) if pair == 0 else jnp.where(left, lat, below)
        before = jnp.where(column == 0, 0.0, pltpu.roll(both, 1, 0))
        after = jnp.where(column == COLS - 1, 0.0, pltpu.roll(both, N_IMG * COLS - 1, 0))
        for odd in range(2):
            parts = [before, both] if odd == 0 else [both, after]
            patch = jnp.concatenate(parts, axis=1).astype(BF16)
            for low in range(2):
                feat_ref[2 * pair + low, odd] = (
                    jnp.dot(
                        patch, wb_ref[odd, :, pl.ds(512 * low, 512)], preferred_element_type=F32
                    )
                    + inb_ref[...]
                ).astype(BF16)
    own = [(1, 0), (1, 1), (2, 0), (2, 1)]
    means, moments = [], []
    for n in range(N_IMG):
        at = pl.ds(n * COLS, COLS)
        total = jnp.zeros((1, 512), F32)
        for h, odd in own:
            total = total + jnp.sum(feat_ref[h, odd, at, :].astype(F32), axis=0, keepdims=True)
        mean = total / 256.0
        moment = jnp.zeros((1, 512), F32)
        for h, odd in own:
            d = feat_ref[h, odd, at, :].astype(F32) - mean
            moment = moment + jnp.sum(d * d, axis=0, keepdims=True)
        means.append(mean)
        moments.append(moment)
    empty = jnp.zeros((4, 512), F32)
    mean4 = jnp.concatenate(means + [empty], axis=0)
    moment4 = jnp.concatenate(moments + [empty], axis=0)
    group = exact_dot(mean4, same_ref[...], NN) / 16.0
    gap = mean4 - group
    moment4 = moment4 + 256.0 * gap * gap
    packed8 = exact_dot(
        jnp.concatenate([mean4[:4], moment4[:4]], axis=0), spread_ref[...], NT
    )
    row8 = lax.broadcasted_iota(jnp.int32, (8, LANES), 0)
    lane8 = lax.broadcasted_iota(jnp.int32, (8, LANES), 1)
    mine = lax.rem(row8, 4) == lax.div(lane8, 32)
    packed8 = jnp.where(mine, packed8, 0.0)
    c1buf[q, 0:1] = jnp.sum(packed8[:4], axis=0, keepdims=True) / 16.0
    c1buf[q, 1:2] = jnp.sum(packed8[4:], axis=0, keepdims=True)
    c1 = []
    for o in range(1, 4):
        c1.append(send(c1buf.at[q], c1buf.at[q], c1_s.at[o - 1], c1_r.at[o - 1], at_q(o)))
    take_y(first)
    for copy in c1:
        copy.wait_recv()

    def merge(buf, count, each):
        centre = buf[0, 0:1]
        for o in range(1, count):
            centre = centre + buf[o, 0:1]
        centre = centre / count
        square = jnp.zeros_like(centre)
        for o in range(count):
            d = buf[o, 0:1] - centre
            square = square + buf[o, 1:2] + each * (d * d)
        return centre, square

    centre, square = merge(c1buf, 4, 4096.0)
    c2buf[z, 0:1] = centre
    c2buf[z, 1:2] = square
    c2 = []
    for o in range(1, nz):
        c2.append(
            send(c2buf.at[z], c2buf.at[z], c2_s.at[o - 1], c2_r.at[o - 1], at_z(zmod(o)))
        )
    take_x(second)
    for copy in c2:
        copy.wait_recv()
    centre, square = merge(c2buf, nz, 4.0 * 4096.0)
    rate = lax.rsqrt(square / (4096.0 * nseq) + 1e-06)
    both8 = jnp.where(mine, jnp.where(row8 < 4, centre, rate), 0.0)
    wide = exact_dot(both8, spread_ref[...], NN)

    first_row = lax.broadcasted_iota(jnp.int32, (COLS, 512), 0)
    keep_top = jnp.where(s == 0, 0.0, 1.0)
    keep_bottom = jnp.where(s == nseq - 1, 0.0, 1.0)
    for n in range(N_IMG):
        at = pl.ds(n * COLS, COLS)
        cen = wide[n : n + 1]
        slope = wide[4 + n : 5 + n] * gain_ref[...]
        for h in range(4):
            for odd in range(2):
                t = (feat_ref[h, odd, at, :].astype(F32) - cen) * slope + shift_ref[...]
                t = 0.5 * t
                act = t + t * jnp.tanh(t)
                if h == 0:
                    act = act * keep_top
                if h == 3:
                    act = act * keep_bottom
                act_ref[h, 1 + odd, at, :] = act.astype(BF16)
                if odd == 0:
                    moved = jnp.where(first_row == COLS - 1, 0.0, pltpu.roll(act, COLS - 1, 0))
                    act_ref[h, 3, at, :] = moved.astype(BF16)
                else:
                    moved = jnp.where(first_row == 0, 0.0, pltpu.roll(act, 1, 0))
                    act_ref[h, 0, at, :] = moved.astype(BF16)
    take_y(second)
    finish_gather()

    for rho in range(2):
        for part in range(2):
            acc = None
            for a in range(3):
                for b in range(3):
                    lhs = act_ref[rho + a, pl.ds(b, 2)].reshape(2 * N_IMG * COLS, 512)
                    term = jnp.dot(
                        lhs,
                        wbuf[part, pl.ds((3 * a + b) * 512, 512), :],
                        preferred_element_type=F32,
                    )
                    acc = term if acc is None else acc + term
            acc = (acc + convb_ref[:, pl.ds(256 * part, 256)]).astype(BF16)
            for odd in range(2):
                for n in range(N_IMG):
                    first = (odd * N_IMG + n) * COLS
                    out_ref[n, rho, :, pl.ds(512 * odd + 256 * part, 256)] = acc[
                        first : first + COLS
                    ]
    for copy in pending:
        copy.wait_send()
    drain()


def on_device(
    nz,
    ngrp,
    conditioning,
    mod_weight,
    mod_bias,
    hidden,
    proj_weight,
    proj_bias,
    noisy_latent,
    in_weight,
    in_bias,
    norm_gain,
    norm_shift,
    conv_weight,
    conv_bias,
):
    width = hidden.shape[2]
    tokens = N_IMG * COLS
    shard = conv_weight.shape[0]
    vmem = pl.BlockSpec(memory_space=pltpu.VMEM)
    hbm = pl.BlockSpec(memory_space=pl.ANY)
    dma = pltpu.SemaphoreType.DMA
    per = nz if ngrp == 2 else 4
    slots = (ngrp // 2) * per + 1
    consts = [jnp.asarray(t) for t in tables()]
    scratch = [
        pltpu.VMEM((N_IMG * ngrp, width), BF16),
        pltpu.VMEM(mod_weight.shape[::-1], BF16),
        pltpu.VMEM((tokens, width), BF16),
        pltpu.VMEM((64, width), BF16),
        pltpu.VMEM((128, 128), BF16),
        pltpu.VMEM(in_weight.shape, BF16),
        pltpu.VMEM((shard, 512), BF16),
        *[pltpu.VMEM(t.shape, BF16) for t in consts],
        pltpu.VMEM((tokens, width), F32),
        pltpu.VMEM((tokens, width), BF16),
        pltpu.VMEM((N_IMG * nz, 512), F32),
        pltpu.VMEM((ngrp, N_IMG, LANES), F32),
        pltpu.VMEM((4, ngrp, N_IMG, LANES), F32),
        pltpu.VMEM((nz, 4 * N_IMG, LANES), BF16),
        pltpu.VMEM((tokens, LANES), F32),
        pltpu.VMEM((tokens, LANES), BF16),
        pltpu.VMEM((2, tokens, LANES), BF16),
        pltpu.VMEM((2, 256, 1024), BF16),
        pltpu.VMEM((4, 2, tokens, 512), BF16),
        pltpu.VMEM((4, 4, tokens, 512), BF16),
        pltpu.VMEM((4, 2, LANES), F32),
        pltpu.VMEM((nz, 2, LANES), F32),
        pltpu.VMEM((2, shard, 256), F32),
        pltpu.VMEM((shard, 256), F32),
        pltpu.VMEM((2, shard * 4 * nz, 256), BF16),
        dma((13,)),
        dma((2,)),
        dma((4 * ngrp - 1,)),
        dma((4 * ngrp - 1,)),
        dma((nz - 1,)),
        dma((nz - 1,)),
        dma((2,)),
        dma((2,)),
        dma((3,)),
        dma((3,)),
        dma((nz - 1,)),
        dma((nz - 1,)),
        dma((per,)),
        dma((per,)),
        dma((ngrp // 2, per)),
        dma((ngrp // 2, per)),
        dma((slots, 2)),
        dma((slots, 2)),
        dma((slots, 2)),
        dma((slots, 2)),
    ]
    out = pl.pallas_call(
        functools.partial(kernel, nz, ngrp),
        out_shape=jax.ShapeDtypeStruct((N_IMG, 2, COLS, 1024), BF16),
        in_specs=[
            vmem if small else hbm
            for small in (0, 0, 1, 0, 0, 1, 0, 0, 1, 1, 1, 0, 1, 0, 0, 0, 0, 0, 0)
        ],
        out_specs=vmem,
        scratch_shapes=scratch,
        compiler_params=pltpu.CompilerParams(
            collective_id=0, has_side_effects=True, vmem_limit_bytes=56 * 1024 * 1024
        ),
    )(
        conditioning,
        mod_weight.T,
        mod_bias.reshape(1, -1),
        hidden.reshape(tokens, width),
        proj_weight.T,
        proj_bias.reshape(1, -1),
        noisy_latent.transpose(0, 1, 3, 2).reshape(128, 128),
        in_weight,
        in_bias.reshape(1, -1),
        norm_gain.reshape(1, -1),
        norm_shift.reshape(1, -1),
        conv_weight,
        conv_bias.reshape(1, -1),
        *consts,
    )
    return out.reshape(N_IMG, 2, 2 * COLS, 512)


def solution(mesh):
    nz = mesh.shape["seq"] // 4
    ngrp = mesh.shape["grp"]
    placed = (
        P(),
        P(None, ("seq", "grp")),
        P(("seq", "grp")),
        P("grp", "seq", None),
        P(),
        P(),
        P("grp", "seq", None, None),
        P(),
        P(),
        P(),
        P(),
        P("seq", None),
        P(),
    )
    return jax.shard_map(
        functools.partial(on_device, nz, ngrp),
        mesh=mesh,
        in_specs=placed,
        out_specs=P("grp", "seq", None, None),
        check_vma=False,
    )
```

```python
import functools

import jax
import jax.numpy as jnp
import ml_dtypes
import numpy as np
from jax import lax
from jax.experimental import pallas as pl
from jax.experimental.pallas import tpu as pltpu
from jax.sharding import PartitionSpec as P

F32 = jnp.float32
BF16 = jnp.bfloat16
NT = (((1,), (1,)), ((), ()))
N_IMG = 4
COLS = 64
LANES = 128


def tables():
    taps = np.zeros((2, 2, 256, 144), np.float32)
    for odd in range(2):
        for low in range(2):
            for block in range(2):
                for down in range(2):
                    for k in range(16):
                        for i in range(2):
                            for j in range(2):
                                a = 2 * down + i - low
                                b = 2 * block + j + odd - 1
                                if 0 <= a <= 2 and 0 <= b <= 2:
                                    row = block * 128 + down * 64 + 4 * k + 2 * i + j
                                    taps[odd, low, row, (3 * a + b) * 16 + k] = 1
    split = np.zeros((128, 128), np.float32)
    for j in range(2):
        for c in range(64):
            split[j * 64 + c, 2 * c + j] = 1
    place = np.zeros((2, 4, 128, 128), np.float32)
    for j in range(2):
        for n in range(4):
            for i in range(2):
                for k in range(16):
                    for twin in range(2):
                        place[j, n, n * 32 + i * 16 + k, twin * 64 + 4 * k + 2 * i + j] = 1
    widen = np.zeros((512, 384), np.float32)
    for q in range(4):
        for l in range(96):
            widen[q * 128 + l, q * 96 + l] = 1
    channel = np.arange(512)
    same = (channel[:, None] // 16 == channel[None, :] // 16).astype(np.float32)
    spread = (np.arange(128)[:, None] % 32 == channel[None, :] // 16).astype(np.float32)
    kinds = (
        taps.reshape(1024, 144),
        split,
        place.reshape(1024, 128),
        widen,
        same,
        spread,
    )
    return [k.astype(ml_dtypes.bfloat16) for k in kinds]


def thirds(x):
    first = x.astype(BF16).astype(F32)
    rest = x - first
    second = rest.astype(BF16).astype(F32)
    third = rest - second
    return jnp.concatenate([first, second, third, jnp.zeros_like(x)], axis=0).astype(BF16)


def exact_dot(x, ones, dims):
    rows = x.shape[0]
    y = lax.dot_general(thirds(x), ones, dims, preferred_element_type=F32)
    return y[:rows] + y[rows : 2 * rows] + y[2 * rows : 3 * rows]


NN = (((1,), (0,)), ((), ()))


def kernel(
    nz,
    ngrp,
    cond_hbm,
    modw_hbm,
    modb_hbm,
    hid_hbm,
    projw_hbm,
    projb_hbm,
    noisy_hbm,
    inw_hbm,
    inb_hbm,
    gain_hbm,
    shift_hbm,
    convw_hbm,
    convb_hbm,
    taps_hbm,
    split_hbm,
    place_hbm,
    widen_hbm,
    same_hbm,
    spread_hbm,
    out_ref,
    cond_ref,
    modw_ref,
    hid_ref,
    projw_ref,
    noisy_ref,
    inw_ref,
    convw_ref,
    taps_ref,
    split_ref,
    place_ref,
    widen_ref,
    same_ref,
    spread_ref,
    modb_ref,
    projb_ref,
    inb_ref,
    gain_ref,
    shift_ref,
    convb_ref,
    xn_ref,
    mod_ref,
    sc_ref,
    a1src,
    a1buf,
    a2buf,
    npk_ref,
    lat_ref,
    halo_ref,
    wb_ref,
    feat_ref,
    act_ref,
    c1buf,
    c2buf,
    stg_ref,
    rcv_ref,
    wbuf,
    ld_sem,
    sw_sem,
    a1_s,
    a1_r,
    a2_s,
    a2_r,
    b_s,
    b_r,
    c1_s,
    c1_r,
    c2_s,
    c2_r,
    z_s,
    z_r,
    x_s,
    x_r,
    y_s,
    y_r,
    k_s,
    k_r,
):
    nseq = 4 * nz
    s = lax.axis_index("seq")
    g = lax.axis_index("grp")
    z = lax.div(s, 4)
    q = lax.rem(s, 4)
    ylo = lax.div(q, 2)
    core = lax.rem(q, 2)
    x = lax.div(g, 2)
    yhi = lax.rem(g, 2)
    yy = 2 * yhi + ylo

    def at_z(zz):
        return {"seq": zz * 4 + q, "grp": g}

    def at_y(step):
        new = lax.rem(yy + 4 + step, 4)
        return {
            "seq": z * 4 + lax.rem(new, 2) * 2 + core,
            "grp": x * 2 + lax.div(new, 2),
        }

    def at_q(o):
        return {"seq": z * 4 + lax.rem(q + o, 4), "grp": g}

    def at_g(o):
        return {"seq": s, "grp": lax.rem(g + o, ngrp)}

    def at_s(step):
        return {"seq": lax.rem(s + nseq + step, nseq), "grp": g}

    mate = {"seq": z * 4 + ylo * 2 + (1 - core), "grp": g}

    def zmod(o):
        return lax.rem(z + nz + o, nz)

    pending = []

    def send(src, dst, ssem, rsem, where):
        copy = pltpu.make_async_remote_copy(
            src_ref=src,
            dst_ref=dst,
            send_sem=ssem,
            recv_sem=rsem,
            device_id=where,
            device_id_type=pl.DeviceIdType.MESH,
        )
        copy.start()
        pending.append(copy)
        return copy

    def at_x(m):
        return {"seq": s, "grp": lax.rem(x + m, ngrp // 2) * 2 + yhi}

    def at_plane(oq, og):
        return {"seq": z * 4 + lax.rem(q + oq, 4), "grp": lax.rem(g + og, ngrp)}

    plane = [(oq, og) for oq in range(4) for og in range(ngrp) if oq or og]
    barrier = pltpu.get_barrier_semaphore()
    greeted = (
        [at_z(zmod(o)) for o in sorted(range(1, nz), key=lambda o: -min(o, nz - o))]
        + [at_plane(oq, og) for oq, og in plane]
        + [at_s(1), at_s(-1)]
    )
    for where in greeted:
        pl.semaphore_signal(barrier, inc=1, device_id=where, device_id_type=pl.DeviceIdType.MESH)

    loads = []
    for i, (src, dst) in enumerate(
        (
            (convw_hbm, convw_ref),
            (cond_hbm, cond_ref),
            (modw_hbm, modw_ref),
            (modb_hbm, modb_ref),
            (hid_hbm, hid_ref),
            (noisy_hbm, noisy_ref),
            (split_hbm, split_ref),
            (place_hbm, place_ref),
            (inw_hbm, inw_ref),
            (taps_hbm, taps_ref),
            (projw_hbm, projw_ref),
            (widen_hbm, widen_ref),
            (same_hbm, same_ref),
            (spread_hbm, spread_ref),
            (projb_hbm, projb_ref),
            (inb_hbm, inb_ref),
            (gain_hbm, gain_ref),
            (shift_hbm, shift_ref),
            (convb_hbm, convb_ref),
        )
    ):
        loads.append(pltpu.make_async_copy(src, dst, ld_sem.at[i]))
        loads[-1].start()

    for copy in loads[:4]:
        copy.wait()
    rows = convw_ref.shape[0]
    whole = convw_ref[...].astype(F32)
    stg_ref[0] = whole[:, :256]
    stg_ref[1] = whole[:, 256:]
    v = cond_ref[...].astype(F32)
    gated = (v / (1.0 + jnp.exp(-v))).astype(BF16)
    own_mod = lax.dot_general(gated, modw_ref[...], NT, preferred_element_type=F32) + modb_ref[...]
    mcols = own_mod.shape[1]
    spot = lax.broadcasted_iota(jnp.int32, (mcols, LANES), 0) + g * mcols
    lane = lax.broadcasted_iota(jnp.int32, (mcols, LANES), 1)
    put = jnp.where(spot == lane, 1.0, 0.0).astype(BF16)
    placed = jnp.dot(own_mod.astype(BF16), put, preferred_element_type=F32)
    for o in range(ngrp):
        a1src[o] = placed[N_IMG * o : N_IMG * (o + 1)]

    pl.semaphore_wait(barrier, len(greeted))

    swap = send(stg_ref.at[1 - core], rcv_ref, sw_sem.at[0], sw_sem.at[1], mate)
    a1 = []
    for i, (oq, og) in enumerate(plane):
        peer = at_plane(oq, og)
        a1.append(send(a1src.at[peer["grp"]], a1buf.at[q, og], a1_s.at[i], a1_r.at[i], peer))

    def chunk(zz, half_y):
        return pl.ds(pl.multiple_of((2 * zz + half_y) * (2 * rows), 16), 2 * rows)

    swap.wait_recv()
    here = stg_ref[core]
    there = rcv_ref[...]
    top = jnp.where(core == 0, here, there)
    bottom = jnp.where(core == 0, there, here)
    block = jnp.concatenate([top, bottom], axis=0).astype(BF16)
    for p in range(2):
        wbuf[p, core, chunk(z, ylo), :] = block[:, 128 * p : 128 * (p + 1)]

    nx = ngrp // 2

    def wanted(j, xx):
        if nx == 1:
            return j
        quarter = nz // 4
        steps = [xx, nz // 2 - xx, nz // 2 + xx, nz - xx][j]
        return jnp.where(xx == 0, quarter * j, steps)

    def guarded(j, xx, act):
        if j == 0:
            pl.when(xx > 0)(act)
        else:
            act()

    per = nz if nx == 1 else 4
    near, far = ([1], [0]) if nx == 1 else ([0, 3], [1, 2])
    def copy_of(src, dst, ssem, rsem, where):
        return pltpu.make_async_remote_copy(
            src_ref=src,
            dst_ref=dst,
            send_sem=ssem,
            recv_sem=rsem,
            device_id=where,
            device_id_type=pl.DeviceIdType.MESH,
        )

    def z_copy(p, j):
        at = wbuf.at[p, core, chunk(z, ylo)]
        where = at_z(lax.rem(z + nz - wanted(j, x), nz))
        return copy_of(at, at, z_s.at[p, j], z_r.at[p, j], where)

    def x_copy(p, m, j):
        at = wbuf.at[p, core, chunk(lax.rem(z + wanted(j, x), nz), ylo)]
        return copy_of(at, at, x_s.at[p, m, j], x_r.at[p, m, j], at_x(m))

    def zz_of(m, j):
        return lax.rem(z + wanted(j, lax.rem(x + nx - m, nx)), nz)

    own_slot = nx * per

    def y_copy(p, slot, zz):
        at = wbuf.at[p, core, chunk(zz, ylo)]
        side = 1 if (slot + p) % 2 == 0 else -1
        return copy_of(at, at, y_s.at[p], y_r.at[p], at_y(side))

    def y_total(p):
        at = wbuf.at[p, core, pl.ds(0, 2 * rows * nz)]
        return copy_of(at, at, y_s.at[p], y_r.at[p], at_y(1))

    def k_copy(p):
        at = wbuf.at[p, core]
        return copy_of(at, at, k_s.at[p], k_r.at[p], mate)

    every = [(m, j) for m in range(nx) for j in range(per)]

    def origin(m):
        return lax.rem(x + nx - m, nx)

    def start_z(p, js):
        for j in js:
            guarded(j, x, lambda j=j: z_copy(p, j).start())

    def onward(p, slot, zz):
        y_copy(p, slot, zz).start()

    def start_own(p):
        onward(p, own_slot, z)

    def take_z(p, js):
        for j in js:

            def act(j=j):
                z_copy(p, j).wait_recv()
                for m in range(1, nx):
                    x_copy(p, m, j).start()
                onward(p, j, zz_of(0, j))

            guarded(j, x, act)

    def take_x(p, js):
        for j in js:
            for m in range(1, nx):

                def act(m=m, j=j):
                    x_copy(p, m, j).wait_recv()
                    onward(p, m * per + j, zz_of(m, j))

                guarded(j, origin(m), act)

    def take_y(p):
        y_total(p).wait_recv()
        k_copy(p).start()

    def finish_gather(p):
        k_copy(p).wait_recv()

    def drain(p):
        for j in range(per):

            def sent(j=j):
                z_copy(p, j).wait_send()
                for m in range(1, nx):
                    x_copy(p, m, j).wait_send()

            guarded(j, x, sent)
        y_total(p).wait_send()
        k_copy(p).wait_send()

    def flush():
        while pending:
            pending.pop().wait_send()

    start_z(0, far + near)
    start_z(1, near)

    for copy in a1:
        copy.wait_recv()
    pieces = []
    for qq in range(4):
        piece = jnp.where(q == qq, a1src[g], jnp.zeros((N_IMG, LANES), F32))
        for og in range(ngrp):
            block = a1buf[qq, og]
            if og == 0:
                block = jnp.where(q == qq, 0.0, block)
            piece = piece + block
        pieces.append(piece)
    a2buf[z] = jnp.concatenate(pieces, axis=0).astype(BF16)
    a2 = []
    for o in sorted(range(1, nz), key=lambda o: -min(o, nz - o)):
        a2.append(
            send(a2buf.at[z], a2buf.at[z], a2_s.at[o - 1], a2_r.at[o - 1], at_z(zmod(o)))
        )

    start_own(0)
    for copy in loads[4:]:
        copy.wait()

    def norm_rows(first, count):
        def body(step, carry):
            at = pl.ds(pl.multiple_of(step * 16, 16), 16)
            h = hid_ref[at, :].astype(F32)
            c = h - jnp.mean(h, axis=-1, keepdims=True)
            var = jnp.mean(c * c, axis=-1, keepdims=True)
            xn_ref[at, :] = c * lax.rsqrt(var + 1e-06)
            return carry

        lax.fori_loop(first, first + count, body, 0)

    norm_rows(0, 8)
    take_z(0, near + far)
    norm_rows(8, 8)
    take_z(1, near)

    de = lax.dot_general(split_ref[...], noisy_ref[...], NT, preferred_element_type=F32).astype(BF16)
    for n in range(N_IMG):
        npk_ref[pl.ds(n * COLS, COLS), :] = jnp.dot(
            de[:64], place_ref[pl.ds(n * 128, 128), :], preferred_element_type=F32
        ) + jnp.dot(de[64:], place_ref[pl.ds(512 + n * 128, 128), :], preferred_element_type=F32)
    for odd in range(2):
        for low in range(2):
            wb_ref[odd, :, pl.ds(512 * low, 512)] = jnp.dot(
                taps_ref[pl.ds((2 * odd + low) * 256, 256), :],
                inw_ref[...],
                preferred_element_type=F32,
            ).astype(BF16)

    for copy in a2:
        copy.wait_recv()
    for zz in range(nz):
        block = a2buf[zz].astype(F32)
        for qq in range(4):
            sc_ref[pl.ds(N_IMG * zz, N_IMG), pl.ds(LANES * qq, LANES)] = block[
                N_IMG * qq : N_IMG * (qq + 1)
            ]
    table = jnp.dot(sc_ref[...].astype(BF16), widen_ref[...], preferred_element_type=F32)
    half = nz // 2
    for n in range(N_IMG):
        for zz in range(half):
            at = (pl.ds(n * COLS, COLS), pl.ds(384 * zz, 384))
            lift = table[N_IMG * zz + n : N_IMG * zz + n + 1]
            move = table[N_IMG * (zz + half) + n : N_IMG * (zz + half) + n + 1]
            mod_ref[at] = (xn_ref[at] * (1.0 + lift) + move).astype(BF16)
    proj = projw_ref[...]
    packed = lax.dot_general(
        mod_ref[...], jnp.concatenate([proj, proj], axis=0), NT, preferred_element_type=F32
    )
    packed = packed + jnp.concatenate([projb_ref[...], projb_ref[...]], axis=1)
    lat_ref[...] = ((npk_ref[...] - 0.75 * packed) / 0.3611 + 0.1159).astype(BF16)
    down = send(lat_ref, halo_ref.at[0], b_s.at[0], b_r.at[0], at_s(1))
    up = send(lat_ref, halo_ref.at[1], b_s.at[1], b_r.at[1], at_s(-1))
    flush()
    down.wait_recv()
    up.wait_recv()
    start_z(1, far)
    lat = lat_ref[...].astype(F32)
    above = jnp.where(s == 0, 0.0, halo_ref[0].astype(F32))
    below = jnp.where(s == nseq - 1, 0.0, halo_ref[1].astype(F32))
    left = lax.broadcasted_iota(jnp.int32, (N_IMG * COLS, LANES), 1) < 64
    column = lax.rem(lax.broadcasted_iota(jnp.int32, (N_IMG * COLS, LANES), 0), COLS)
    for pair in range(2):
        both = jnp.where(left, above, lat) if pair == 0 else jnp.where(left, lat, below)
        before = jnp.where(column == 0, 0.0, pltpu.roll(both, 1, 0))
        after = jnp.where(column == COLS - 1, 0.0, pltpu.roll(both, N_IMG * COLS - 1, 0))
        for odd in range(2):
            parts = [before, both] if odd == 0 else [both, after]
            patch = jnp.concatenate(parts, axis=1).astype(BF16)
            for low in range(2):
                feat_ref[2 * pair + low, odd] = (
                    jnp.dot(
                        patch, wb_ref[odd, :, pl.ds(512 * low, 512)], preferred_element_type=F32
                    )
                    + inb_ref[...]
                ).astype(BF16)
    own = [(1, 0), (1, 1), (2, 0), (2, 1)]
    means, moments = [], []
    for n in range(N_IMG):
        at = pl.ds(n * COLS, COLS)
        total = jnp.zeros((1, 512), F32)
        for h, odd in own:
            total = total + jnp.sum(feat_ref[h, odd, at, :].astype(F32), axis=0, keepdims=True)
        mean = total / 256.0
        moment = jnp.zeros((1, 512), F32)
        for h, odd in own:
            d = feat_ref[h, odd, at, :].astype(F32) - mean
            moment = moment + jnp.sum(d * d, axis=0, keepdims=True)
        means.append(mean)
        moments.append(moment)
    empty = jnp.zeros((4, 512), F32)
    mean4 = jnp.concatenate(means + [empty], axis=0)
    moment4 = jnp.concatenate(moments + [empty], axis=0)
    group = exact_dot(mean4, same_ref[...], NN) / 16.0
    gap = mean4 - group
    moment4 = moment4 + 256.0 * gap * gap
    packed8 = exact_dot(
        jnp.concatenate([mean4[:4], moment4[:4]], axis=0), spread_ref[...], NT
    )
    row8 = lax.broadcasted_iota(jnp.int32, (8, LANES), 0)
    lane8 = lax.broadcasted_iota(jnp.int32, (8, LANES), 1)
    mine = lax.rem(row8, 4) == lax.div(lane8, 32)
    packed8 = jnp.where(mine, packed8, 0.0)
    c1buf[q, 0:1] = jnp.sum(packed8[:4], axis=0, keepdims=True) / 16.0
    c1buf[q, 1:2] = jnp.sum(packed8[4:], axis=0, keepdims=True)
    c1 = []
    for o in range(1, 4):
        c1.append(send(c1buf.at[q], c1buf.at[q], c1_s.at[o - 1], c1_r.at[o - 1], at_q(o)))
    for copy in c1:
        copy.wait_recv()

    def merge(buf, count, each):
        centre = buf[0, 0:1]
        for o in range(1, count):
            centre = centre + buf[o, 0:1]
        centre = centre / count
        square = jnp.zeros_like(centre)
        for o in range(count):
            d = buf[o, 0:1] - centre
            square = square + buf[o, 1:2] + each * (d * d)
        return centre, square

    centre, square = merge(c1buf, 4, 4096.0)
    c2buf[z, 0:1] = centre
    c2buf[z, 1:2] = square
    c2 = []
    for o in range(1, nz):
        c2.append(
            send(c2buf.at[z], c2buf.at[z], c2_s.at[o - 1], c2_r.at[o - 1], at_z(zmod(o)))
        )
    take_x(0, near + far)
    start_own(1)
    take_x(1, near)
    take_z(1, far)
    take_y(0)
    take_x(1, far)
    for copy in c2:
        copy.wait_recv()
    centre, square = merge(c2buf, nz, 4.0 * 4096.0)
    rate = lax.rsqrt(square / (4096.0 * nseq) + 1e-06)
    both8 = jnp.where(mine, jnp.where(row8 < 4, centre, rate), 0.0)
    wide = exact_dot(both8, spread_ref[...], NN)

    first_row = lax.broadcasted_iota(jnp.int32, (COLS, 512), 0)
    keep_top = jnp.where(s == 0, 0.0, 1.0)
    keep_bottom = jnp.where(s == nseq - 1, 0.0, 1.0)
    for n in range(N_IMG):
        at = pl.ds(n * COLS, COLS)
        cen = wide[n : n + 1]
        slope = wide[4 + n : 5 + n] * gain_ref[...]
        for h in range(4):
            for odd in range(2):
                t = (feat_ref[h, odd, at, :].astype(F32) - cen) * slope + shift_ref[...]
                t = 0.5 * t
                act = t + t * jnp.tanh(t)
                if h == 0:
                    act = act * keep_top
                if h == 3:
                    act = act * keep_bottom
                act_ref[h, 1 + odd, at, :] = act.astype(BF16)
                if odd == 0:
                    moved = jnp.where(first_row == COLS - 1, 0.0, pltpu.roll(act, COLS - 1, 0))
                    act_ref[h, 3, at, :] = moved.astype(BF16)
                else:
                    moved = jnp.where(first_row == 0, 0.0, pltpu.roll(act, 1, 0))
                    act_ref[h, 0, at, :] = moved.astype(BF16)
    flush()
    finish_gather(0)
    drain(0)

    for p in range(2):
        bias = jnp.concatenate(
            [convb_ref[:, pl.ds(128 * p, 128)], convb_ref[:, pl.ds(256 + 128 * p, 128)]], axis=1
        )
        for rho in range(2):
            acc = None
            for a in range(3):
                for b in range(3):
                    lhs = act_ref[rho + a, pl.ds(b, 2)].reshape(2 * N_IMG * COLS, 512)
                    depth = pl.ds((3 * a + b) * 512, 512)
                    rhs = jnp.concatenate([wbuf[p, 0, depth, :], wbuf[p, 1, depth, :]], axis=1)
                    term = jnp.dot(lhs, rhs, preferred_element_type=F32)
                    acc = term if acc is None else acc + term
            acc = (acc + bias).astype(BF16)
            for odd in range(2):
                for n in range(N_IMG):
                    row = (odd * N_IMG + n) * COLS
                    for part in range(2):
                        at = pl.ds(512 * odd + 256 * part + 128 * p, 128)
                        out_ref[n, rho, :, at] = acc[
                            row : row + COLS, 128 * part : 128 * (part + 1)
                        ]
            if p == 0 and rho == 0:
                take_y(1)
            if p == 0 and rho == 1:
                finish_gather(1)
    drain(1)


def on_device(
    nz,
    ngrp,
    conditioning,
    mod_weight,
    mod_bias,
    hidden,
    proj_weight,
    proj_bias,
    noisy_latent,
    in_weight,
    in_bias,
    norm_gain,
    norm_shift,
    conv_weight,
    conv_bias,
):
    width = hidden.shape[2]
    tokens = N_IMG * COLS
    shard = conv_weight.shape[0]
    vmem = pl.BlockSpec(memory_space=pltpu.VMEM)
    hbm = pl.BlockSpec(memory_space=pl.ANY)
    dma = pltpu.SemaphoreType.DMA
    per = nz if ngrp == 2 else 4
    consts = [jnp.asarray(t) for t in tables()]
    scratch = [
        pltpu.VMEM((N_IMG * ngrp, width), BF16),
        pltpu.VMEM(mod_weight.shape[::-1], BF16),
        pltpu.VMEM((tokens, width), BF16),
        pltpu.VMEM((64, width), BF16),
        pltpu.VMEM((128, 128), BF16),
        pltpu.VMEM(in_weight.shape, BF16),
        pltpu.VMEM((shard, 512), BF16),
        *[pltpu.VMEM(t.shape, BF16) for t in consts],
        *[pltpu.VMEM((1, n), F32) for n in (mod_weight.shape[1], 64, 512, 512, 512, 512)],
        pltpu.VMEM((tokens, width), F32),
        pltpu.VMEM((tokens, width), BF16),
        pltpu.VMEM((N_IMG * nz, 512), F32),
        pltpu.VMEM((ngrp, N_IMG, LANES), F32),
        pltpu.VMEM((4, ngrp, N_IMG, LANES), F32),
        pltpu.VMEM((nz, 4 * N_IMG, LANES), BF16),
        pltpu.VMEM((tokens, LANES), F32),
        pltpu.VMEM((tokens, LANES), BF16),
        pltpu.VMEM((2, tokens, LANES), BF16),
        pltpu.VMEM((2, 256, 1024), BF16),
        pltpu.VMEM((4, 2, tokens, 512), BF16),
        pltpu.VMEM((4, 4, tokens, 512), BF16),
        pltpu.VMEM((4, 2, LANES), F32),
        pltpu.VMEM((nz, 2, LANES), F32),
        pltpu.VMEM((2, shard, 256), F32),
        pltpu.VMEM((shard, 256), F32),
        pltpu.VMEM((2, 2, shard * 4 * nz, 128), BF16),
        dma((19,)),
        dma((2,)),
        dma((4 * ngrp - 1,)),
        dma((4 * ngrp - 1,)),
        dma((nz - 1,)),
        dma((nz - 1,)),
        dma((2,)),
        dma((2,)),
        dma((3,)),
        dma((3,)),
        dma((nz - 1,)),
        dma((nz - 1,)),
        dma((2, per)),
        dma((2, per)),
        dma((2, ngrp // 2, per)),
        dma((2, ngrp // 2, per)),
        dma((2,)),
        dma((2,)),
        dma((2,)),
        dma((2,)),
    ]
    out = pl.pallas_call(
        functools.partial(kernel, nz, ngrp),
        out_shape=jax.ShapeDtypeStruct((N_IMG, 2, COLS, 1024), BF16),
        in_specs=[hbm] * 19,
        out_specs=vmem,
        scratch_shapes=scratch,
        compiler_params=pltpu.CompilerParams(
            collective_id=0, has_side_effects=True, vmem_limit_bytes=56 * 1024 * 1024
        ),
    )(
        conditioning,
        mod_weight.T,
        mod_bias.reshape(1, -1),
        hidden.reshape(tokens, width),
        proj_weight.T,
        proj_bias.reshape(1, -1),
        noisy_latent.transpose(0, 1, 3, 2).reshape(128, 128),
        in_weight,
        in_bias.reshape(1, -1),
        norm_gain.reshape(1, -1),
        norm_shift.reshape(1, -1),
        conv_weight,
        conv_bias.reshape(1, -1),
        *consts,
    )
    return out.reshape(N_IMG, 2, 2 * COLS, 512)


def solution(mesh):
    nz = mesh.shape["seq"] // 4
    ngrp = mesh.shape["grp"]
    placed = (
        P(),
        P(None, ("seq", "grp")),
        P(("seq", "grp")),
        P("grp", "seq", None),
        P(),
        P(),
        P("grp", "seq", None, None),
        P(),
        P(),
        P(),
        P(),
        P("seq", None),
        P(),
    )
    return jax.shard_map(
        functools.partial(on_device, nz, ngrp),
        mesh=mesh,
        in_specs=placed,
        out_specs=P("grp", "seq", None, None),
        check_vma=False,
    )
```

```python
import functools

import jax
import jax.numpy as jnp
import ml_dtypes
import numpy as np
from jax import lax
from jax.experimental import pallas as pl
from jax.experimental.pallas import tpu as pltpu
from jax.sharding import PartitionSpec as P

F32 = jnp.float32
BF16 = jnp.bfloat16
NT = (((1,), (1,)), ((), ()))
N_IMG = 4
COLS = 64
LANES = 128


def tables():
    taps = np.zeros((2, 2, 256, 144), np.float32)
    for odd in range(2):
        for low in range(2):
            for block in range(2):
                for down in range(2):
                    for k in range(16):
                        for i in range(2):
                            for j in range(2):
                                a = 2 * down + i - low
                                b = 2 * block + j + odd - 1
                                if 0 <= a <= 2 and 0 <= b <= 2:
                                    row = block * 128 + down * 64 + 4 * k + 2 * i + j
                                    taps[odd, low, row, (3 * a + b) * 16 + k] = 1
    split = np.zeros((128, 128), np.float32)
    for j in range(2):
        for c in range(64):
            split[j * 64 + c, 2 * c + j] = 1
    place = np.zeros((2, 4, 128, 128), np.float32)
    for j in range(2):
        for n in range(4):
            for i in range(2):
                for k in range(16):
                    for twin in range(2):
                        place[j, n, n * 32 + i * 16 + k, twin * 64 + 4 * k + 2 * i + j] = 1
    widen = np.zeros((512, 384), np.float32)
    for q in range(4):
        for l in range(96):
            widen[q * 128 + l, q * 96 + l] = 1
    channel = np.arange(512)
    same = (channel[:, None] // 16 == channel[None, :] // 16).astype(np.float32)
    spread = (np.arange(128)[:, None] % 32 == channel[None, :] // 16).astype(np.float32)
    kinds = (
        taps.reshape(1024, 144),
        split,
        place.reshape(1024, 128),
        widen,
        same,
        spread,
    )
    return [k.astype(ml_dtypes.bfloat16) for k in kinds]


def thirds(x):
    first = x.astype(BF16).astype(F32)
    rest = x - first
    second = rest.astype(BF16).astype(F32)
    third = rest - second
    return jnp.concatenate([first, second, third, jnp.zeros_like(x)], axis=0).astype(BF16)


def exact_dot(x, ones, dims):
    rows = x.shape[0]
    y = lax.dot_general(thirds(x), ones, dims, preferred_element_type=F32)
    return y[:rows] + y[rows : 2 * rows] + y[2 * rows : 3 * rows]


NN = (((1,), (0,)), ((), ()))


def kernel(
    nz,
    ngrp,
    cond_hbm,
    modw_hbm,
    modb_hbm,
    hid_hbm,
    projw_hbm,
    projb_hbm,
    noisy_hbm,
    inw_hbm,
    inb_hbm,
    gain_hbm,
    shift_hbm,
    convw_hbm,
    convb_hbm,
    taps_hbm,
    split_hbm,
    place_hbm,
    widen_hbm,
    same_hbm,
    spread_hbm,
    out_ref,
    cond_ref,
    modw_ref,
    hid_ref,
    projw_ref,
    noisy_ref,
    inw_ref,
    convw_ref,
    taps_ref,
    split_ref,
    place_ref,
    widen_ref,
    same_ref,
    spread_ref,
    modb_ref,
    projb_ref,
    inb_ref,
    gain_ref,
    shift_ref,
    convb_ref,
    xn_ref,
    mod_ref,
    sc_ref,
    a1src,
    a1buf,
    a2buf,
    npk_ref,
    lat_ref,
    halo_ref,
    wb_ref,
    feat_ref,
    act_ref,
    c1buf,
    c2buf,
    stg_ref,
    rcv_ref,
    wbuf,
    ld_sem,
    sw_sem,
    a1_s,
    a1_r,
    a2_s,
    a2_r,
    b_s,
    b_r,
    c1_s,
    c1_r,
    c2_s,
    c2_r,
    z_s,
    z_r,
    x_s,
    x_r,
    y_s,
    y_r,
    k_s,
    k_r,
):
    nseq = 4 * nz
    s = lax.axis_index("seq")
    g = lax.axis_index("grp")
    z = lax.div(s, 4)
    q = lax.rem(s, 4)
    ylo = lax.div(q, 2)
    core = lax.rem(q, 2)
    x = lax.div(g, 2)
    yhi = lax.rem(g, 2)
    yy = 2 * yhi + ylo

    def at_z(zz):
        return {"seq": zz * 4 + q, "grp": g}

    def at_y(step):
        new = lax.rem(yy + 4 + step, 4)
        return {
            "seq": z * 4 + lax.rem(new, 2) * 2 + core,
            "grp": x * 2 + lax.div(new, 2),
        }

    def at_q(o):
        return {"seq": z * 4 + lax.rem(q + o, 4), "grp": g}

    def at_g(o):
        return {"seq": s, "grp": lax.rem(g + o, ngrp)}

    def at_s(step):
        return {"seq": lax.rem(s + nseq + step, nseq), "grp": g}

    mate = {"seq": z * 4 + ylo * 2 + (1 - core), "grp": g}

    def zmod(o):
        return lax.rem(z + nz + o, nz)

    pending = []

    def send(src, dst, ssem, rsem, where):
        copy = pltpu.make_async_remote_copy(
            src_ref=src,
            dst_ref=dst,
            send_sem=ssem,
            recv_sem=rsem,
            device_id=where,
            device_id_type=pl.DeviceIdType.MESH,
        )
        copy.start()
        pending.append(copy)
        return copy

    def at_x(m):
        return {"seq": s, "grp": lax.rem(x + m, ngrp // 2) * 2 + yhi}

    def at_plane(oq, og):
        return {"seq": z * 4 + lax.rem(q + oq, 4), "grp": lax.rem(g + og, ngrp)}

    plane = [(oq, og) for oq in range(4) for og in range(ngrp) if oq or og]
    barrier = pltpu.get_barrier_semaphore()
    greeted = (
        [at_z(zmod(o)) for o in sorted(range(1, nz), key=lambda o: -min(o, nz - o))]
        + [at_plane(oq, og) for oq, og in plane]
        + [at_s(1), at_s(-1)]
    )
    for where in greeted:
        pl.semaphore_signal(barrier, inc=1, device_id=where, device_id_type=pl.DeviceIdType.MESH)

    loads = []
    for i, (src, dst) in enumerate(
        (
            (convw_hbm, convw_ref),
            (cond_hbm, cond_ref),
            (modw_hbm, modw_ref),
            (modb_hbm, modb_ref),
            (hid_hbm, hid_ref),
            (noisy_hbm, noisy_ref),
            (split_hbm, split_ref),
            (place_hbm, place_ref),
            (inw_hbm, inw_ref),
            (taps_hbm, taps_ref),
            (projw_hbm, projw_ref),
            (widen_hbm, widen_ref),
            (same_hbm, same_ref),
            (spread_hbm, spread_ref),
            (projb_hbm, projb_ref),
            (inb_hbm, inb_ref),
            (gain_hbm, gain_ref),
            (shift_hbm, shift_ref),
            (convb_hbm, convb_ref),
        )
    ):
        loads.append(pltpu.make_async_copy(src, dst, ld_sem.at[i]))
        loads[-1].start()

    for copy in loads[:4]:
        copy.wait()
    rows = convw_ref.shape[0]
    whole = convw_ref[...].astype(F32)
    stg_ref[0] = whole[:, :256]
    stg_ref[1] = whole[:, 256:]
    v = cond_ref[...].astype(F32)
    gated = (v / (1.0 + jnp.exp(-v))).astype(BF16)
    own_mod = lax.dot_general(gated, modw_ref[...], NT, preferred_element_type=F32) + modb_ref[...]
    mcols = own_mod.shape[1]
    spot = lax.broadcasted_iota(jnp.int32, (mcols, LANES), 0) + g * mcols
    lane = lax.broadcasted_iota(jnp.int32, (mcols, LANES), 1)
    put = jnp.where(spot == lane, 1.0, 0.0).astype(BF16)
    placed = jnp.dot(own_mod.astype(BF16), put, preferred_element_type=F32)
    for o in range(ngrp):
        a1src[o] = placed[N_IMG * o : N_IMG * (o + 1)]

    pl.semaphore_wait(barrier, len(greeted))

    swap = send(stg_ref.at[1 - core], rcv_ref, sw_sem.at[0], sw_sem.at[1], mate)
    a1 = []
    for i, (oq, og) in enumerate(plane):
        peer = at_plane(oq, og)
        a1.append(send(a1src.at[peer["grp"]], a1buf.at[q, og], a1_s.at[i], a1_r.at[i], peer))

    def chunk(zz, half_y):
        return pl.ds(pl.multiple_of((2 * zz + half_y) * (2 * rows), 16), 2 * rows)

    swap.wait_recv()
    here = stg_ref[core]
    there = rcv_ref[...]
    top = jnp.where(core == 0, here, there)
    bottom = jnp.where(core == 0, there, here)
    block = jnp.concatenate([top, bottom], axis=0).astype(BF16)
    for p in range(2):
        wbuf[p, core, chunk(z, ylo), :] = block[:, 128 * p : 128 * (p + 1)]

    nx = ngrp // 2

    def wanted(j, xx):
        if nx == 1:
            return j
        quarter = nz // 4
        steps = [xx, nz // 2 - xx, nz // 2 + xx, nz - xx][j]
        return jnp.where(xx == 0, quarter * j, steps)

    def guarded(j, xx, act):
        if j == 0:
            pl.when(xx > 0)(act)
        else:
            act()

    per = nz if nx == 1 else 4
    near, far = ([1], [0]) if nx == 1 else ([0, 3], [1, 2])
    def copy_of(src, dst, ssem, rsem, where):
        return pltpu.make_async_remote_copy(
            src_ref=src,
            dst_ref=dst,
            send_sem=ssem,
            recv_sem=rsem,
            device_id=where,
            device_id_type=pl.DeviceIdType.MESH,
        )

    def z_copy(p, j):
        at = wbuf.at[p, core, chunk(z, ylo)]
        where = at_z(lax.rem(z + nz - wanted(j, x), nz))
        return copy_of(at, at, z_s.at[p, j], z_r.at[p, j], where)

    def x_copy(p, m, j):
        at = wbuf.at[p, core, chunk(lax.rem(z + wanted(j, x), nz), ylo)]
        return copy_of(at, at, x_s.at[p, m, j], x_r.at[p, m, j], at_x(m))

    def zz_of(m, j):
        return lax.rem(z + wanted(j, lax.rem(x + nx - m, nx)), nz)

    own_slot = nx * per

    def y_copy(p, slot, zz):
        at = wbuf.at[p, core, chunk(zz, ylo)]
        side = 1 if (slot + p) % 2 == 0 else -1
        return copy_of(at, at, y_s.at[p], y_r.at[p], at_y(side))

    def y_total(p):
        at = wbuf.at[p, core, pl.ds(0, 2 * rows * nz)]
        return copy_of(at, at, y_s.at[p], y_r.at[p], at_y(1))

    def k_copy(p):
        at = wbuf.at[p, core]
        return copy_of(at, at, k_s.at[p], k_r.at[p], mate)

    every = [(m, j) for m in range(nx) for j in range(per)]

    def origin(m):
        return lax.rem(x + nx - m, nx)

    def start_z(p, js):
        for j in js:
            guarded(j, x, lambda j=j: z_copy(p, j).start())

    def onward(p, slot, zz):
        y_copy(p, slot, zz).start()

    def start_own(p):
        onward(p, own_slot, z)

    def take_z(p, js):
        for j in js:

            def act(j=j):
                z_copy(p, j).wait_recv()
                for m in range(1, nx):
                    x_copy(p, m, j).start()
                onward(p, j, zz_of(0, j))

            guarded(j, x, act)

    def take_x(p, js):
        for j in js:
            for m in range(1, nx):

                def act(m=m, j=j):
                    x_copy(p, m, j).wait_recv()
                    onward(p, m * per + j, zz_of(m, j))

                guarded(j, origin(m), act)

    def take_y(p):
        y_total(p).wait_recv()
        k_copy(p).start()

    def finish_gather(p):
        k_copy(p).wait_recv()

    def drain(p):
        for j in range(per):

            def sent(j=j):
                z_copy(p, j).wait_send()
                for m in range(1, nx):
                    x_copy(p, m, j).wait_send()

            guarded(j, x, sent)
        y_total(p).wait_send()
        k_copy(p).wait_send()

    def flush():
        while pending:
            pending.pop().wait_send()

    start_z(0, near)
    start_z(0, far)

    for copy in loads[4:]:
        copy.wait()

    def norm_rows(first, count):
        def body(step, carry):
            at = pl.ds(pl.multiple_of(step * 16, 16), 16)
            h = hid_ref[at, :].astype(F32)
            c = h - jnp.mean(h, axis=-1, keepdims=True)
            var = jnp.mean(c * c, axis=-1, keepdims=True)
            xn_ref[at, :] = c * lax.rsqrt(var + 1e-06)
            return carry

        lax.fori_loop(first, first + count, body, 0)

    norm_rows(0, 16)

    de = lax.dot_general(split_ref[...], noisy_ref[...], NT, preferred_element_type=F32).astype(BF16)
    for n in range(N_IMG):
        npk_ref[pl.ds(n * COLS, COLS), :] = jnp.dot(
            de[:64], place_ref[pl.ds(n * 128, 128), :], preferred_element_type=F32
        ) + jnp.dot(de[64:], place_ref[pl.ds(512 + n * 128, 128), :], preferred_element_type=F32)

    for copy in a1:
        copy.wait_recv()
    pieces = []
    for qq in range(4):
        piece = jnp.where(q == qq, a1src[g], jnp.zeros((N_IMG, LANES), F32))
        for og in range(ngrp):
            block = a1buf[qq, og]
            if og == 0:
                block = jnp.where(q == qq, 0.0, block)
            piece = piece + block
        pieces.append(piece)
    a2buf[z] = jnp.concatenate(pieces, axis=0).astype(BF16)
    a2 = []
    for o in sorted(range(1, nz), key=lambda o: -min(o, nz - o)):
        a2.append(
            send(a2buf.at[z], a2buf.at[z], a2_s.at[o - 1], a2_r.at[o - 1], at_z(zmod(o)))
        )

    start_own(0)
    take_z(0, near)
    for odd in range(2):
        for low in range(2):
            wb_ref[odd, :, pl.ds(512 * low, 512)] = jnp.dot(
                taps_ref[pl.ds((2 * odd + low) * 256, 256), :],
                inw_ref[...],
                preferred_element_type=F32,
            ).astype(BF16)

    take_x(0, near)
    take_z(0, far)
    for copy in a2:
        copy.wait_recv()
    for zz in range(nz):
        block = a2buf[zz].astype(F32)
        for qq in range(4):
            sc_ref[pl.ds(N_IMG * zz, N_IMG), pl.ds(LANES * qq, LANES)] = block[
                N_IMG * qq : N_IMG * (qq + 1)
            ]
    table = jnp.dot(sc_ref[...].astype(BF16), widen_ref[...], preferred_element_type=F32)
    half = nz // 2
    for n in range(N_IMG):
        for zz in range(half):
            at = (pl.ds(n * COLS, COLS), pl.ds(384 * zz, 384))
            lift = table[N_IMG * zz + n : N_IMG * zz + n + 1]
            move = table[N_IMG * (zz + half) + n : N_IMG * (zz + half) + n + 1]
            mod_ref[at] = (xn_ref[at] * (1.0 + lift) + move).astype(BF16)
    proj = projw_ref[...]
    packed = lax.dot_general(
        mod_ref[...], jnp.concatenate([proj, proj], axis=0), NT, preferred_element_type=F32
    )
    packed = packed + jnp.concatenate([projb_ref[...], projb_ref[...]], axis=1)
    lat_ref[...] = ((npk_ref[...] - 0.75 * packed) / 0.3611 + 0.1159).astype(BF16)
    down = send(lat_ref, halo_ref.at[0], b_s.at[0], b_r.at[0], at_s(1))
    up = send(lat_ref, halo_ref.at[1], b_s.at[1], b_r.at[1], at_s(-1))
    start_z(1, near)
    start_z(1, far)
    flush()
    down.wait_recv()
    up.wait_recv()
    take_x(0, far)
    start_own(1)
    lat = lat_ref[...].astype(F32)
    above = jnp.where(s == 0, 0.0, halo_ref[0].astype(F32))
    below = jnp.where(s == nseq - 1, 0.0, halo_ref[1].astype(F32))
    left = lax.broadcasted_iota(jnp.int32, (N_IMG * COLS, LANES), 1) < 64
    column = lax.rem(lax.broadcasted_iota(jnp.int32, (N_IMG * COLS, LANES), 0), COLS)
    patches = {}
    for pair in range(2):
        both = jnp.where(left, above, lat) if pair == 0 else jnp.where(left, lat, below)
        before = jnp.where(column == 0, 0.0, pltpu.roll(both, 1, 0))
        after = jnp.where(column == COLS - 1, 0.0, pltpu.roll(both, N_IMG * COLS - 1, 0))
        for odd in range(2):
            parts = [before, both] if odd == 0 else [both, after]
            patches[pair, odd] = jnp.concatenate(parts, axis=1).astype(BF16)

    def make_features(pair, low):
        for odd in range(2):
            feat_ref[2 * pair + low, odd] = (
                jnp.dot(
                    patches[pair, odd],
                    wb_ref[odd, :, pl.ds(512 * low, 512)],
                    preferred_element_type=F32,
                )
                + inb_ref[...]
            ).astype(BF16)

    make_features(0, 1)
    make_features(1, 0)

    own = [(1, 0), (1, 1), (2, 0), (2, 1)]
    means, moments = [], []
    for n in range(N_IMG):
        at = pl.ds(n * COLS, COLS)
        total = jnp.zeros((1, 512), F32)
        for h, odd in own:
            total = total + jnp.sum(feat_ref[h, odd, at, :].astype(F32), axis=0, keepdims=True)
        mean = total / 256.0
        moment = jnp.zeros((1, 512), F32)
        for h, odd in own:
            d = feat_ref[h, odd, at, :].astype(F32) - mean
            moment = moment + jnp.sum(d * d, axis=0, keepdims=True)
        means.append(mean)
        moments.append(moment)
    empty = jnp.zeros((4, 512), F32)
    mean4 = jnp.concatenate(means + [empty], axis=0)
    moment4 = jnp.concatenate(moments + [empty], axis=0)
    group = exact_dot(mean4, same_ref[...], NN) / 16.0
    gap = mean4 - group
    moment4 = moment4 + 256.0 * gap * gap
    packed8 = exact_dot(
        jnp.concatenate([mean4[:4], moment4[:4]], axis=0), spread_ref[...], NT
    )
    row8 = lax.broadcasted_iota(jnp.int32, (8, LANES), 0)
    lane8 = lax.broadcasted_iota(jnp.int32, (8, LANES), 1)
    mine = lax.rem(row8, 4) == lax.div(lane8, 32)
    packed8 = jnp.where(mine, packed8, 0.0)
    c1buf[q, 0:1] = jnp.sum(packed8[:4], axis=0, keepdims=True) / 16.0
    c1buf[q, 1:2] = jnp.sum(packed8[4:], axis=0, keepdims=True)
    c1 = []
    for o in range(1, 4):
        c1.append(send(c1buf.at[q], c1buf.at[q], c1_s.at[o - 1], c1_r.at[o - 1], at_q(o)))
    take_z(1, near)
    make_features(0, 0)
    make_features(1, 1)
    for copy in c1:
        copy.wait_recv()

    def merge(buf, count, each):
        centre = buf[0, 0:1]
        for o in range(1, count):
            centre = centre + buf[o, 0:1]
        centre = centre / count
        square = jnp.zeros_like(centre)
        for o in range(count):
            d = buf[o, 0:1] - centre
            square = square + buf[o, 1:2] + each * (d * d)
        return centre, square

    centre, square = merge(c1buf, 4, 4096.0)
    c2buf[z, 0:1] = centre
    c2buf[z, 1:2] = square
    c2 = []
    for o in range(1, nz):
        c2.append(
            send(c2buf.at[z], c2buf.at[z], c2_s.at[o - 1], c2_r.at[o - 1], at_z(zmod(o)))
        )
    take_z(1, far)
    take_x(1, near)
    take_x(1, far)
    take_y(0)
    for copy in c2:
        copy.wait_recv()
    centre, square = merge(c2buf, nz, 4.0 * 4096.0)
    rate = lax.rsqrt(square / (4096.0 * nseq) + 1e-06)
    both8 = jnp.where(mine, jnp.where(row8 < 4, centre, rate), 0.0)
    wide = exact_dot(both8, spread_ref[...], NN)

    first_row = lax.broadcasted_iota(jnp.int32, (COLS, 512), 0)
    keep_top = jnp.where(s == 0, 0.0, 1.0)
    keep_bottom = jnp.where(s == nseq - 1, 0.0, 1.0)
    for n in range(N_IMG):
        at = pl.ds(n * COLS, COLS)
        cen = wide[n : n + 1]
        slope = wide[4 + n : 5 + n] * gain_ref[...]
        for h in range(4):
            for odd in range(2):
                t = (feat_ref[h, odd, at, :].astype(F32) - cen) * slope + shift_ref[...]
                t = 0.5 * t
                act = t + t * jnp.tanh(t)
                if h == 0:
                    act = act * keep_top
                if h == 3:
                    act = act * keep_bottom
                act_ref[h, 1 + odd, at, :] = act.astype(BF16)
                if odd == 0:
                    moved = jnp.where(first_row == COLS - 1, 0.0, pltpu.roll(act, COLS - 1, 0))
                    act_ref[h, 3, at, :] = moved.astype(BF16)
                else:
                    moved = jnp.where(first_row == 0, 0.0, pltpu.roll(act, 1, 0))
                    act_ref[h, 0, at, :] = moved.astype(BF16)
    flush()
    finish_gather(0)
    drain(0)

    for p in range(2):
        bias = jnp.concatenate(
            [convb_ref[:, pl.ds(128 * p, 128)], convb_ref[:, pl.ds(256 + 128 * p, 128)]], axis=1
        )
        for rho in range(2):
            acc = None
            for a in range(3):
                for b in range(3):
                    lhs = act_ref[rho + a, pl.ds(b, 2)].reshape(2 * N_IMG * COLS, 512)
                    depth = pl.ds((3 * a + b) * 512, 512)
                    rhs = jnp.concatenate([wbuf[p, 0, depth, :], wbuf[p, 1, depth, :]], axis=1)
                    term = jnp.dot(lhs, rhs, preferred_element_type=F32)
                    acc = term if acc is None else acc + term
            acc = (acc + bias).astype(BF16)
            for odd in range(2):
                for n in range(N_IMG):
                    row = (odd * N_IMG + n) * COLS
                    for part in range(2):
                        at = pl.ds(512 * odd + 256 * part + 128 * p, 128)
                        out_ref[n, rho, :, at] = acc[
                            row : row + COLS, 128 * part : 128 * (part + 1)
                        ]
            if p == 0 and rho == 0:
                take_y(1)
            if p == 0 and rho == 1:
                finish_gather(1)
    drain(1)


def on_device(
    nz,
    ngrp,
    conditioning,
    mod_weight,
    mod_bias,
    hidden,
    proj_weight,
    proj_bias,
    noisy_latent,
    in_weight,
    in_bias,
    norm_gain,
    norm_shift,
    conv_weight,
    conv_bias,
):
    width = hidden.shape[2]
    tokens = N_IMG * COLS
    shard = conv_weight.shape[0]
    vmem = pl.BlockSpec(memory_space=pltpu.VMEM)
    hbm = pl.BlockSpec(memory_space=pl.ANY)
    dma = pltpu.SemaphoreType.DMA
    per = nz if ngrp == 2 else 4
    consts = [jnp.asarray(t) for t in tables()]
    scratch = [
        pltpu.VMEM((N_IMG * ngrp, width), BF16),
        pltpu.VMEM(mod_weight.shape[::-1], BF16),
        pltpu.VMEM((tokens, width), BF16),
        pltpu.VMEM((64, width), BF16),
        pltpu.VMEM((128, 128), BF16),
        pltpu.VMEM(in_weight.shape, BF16),
        pltpu.VMEM((shard, 512), BF16),
        *[pltpu.VMEM(t.shape, BF16) for t in consts],
        *[pltpu.VMEM((1, n), F32) for n in (mod_weight.shape[1], 64, 512, 512, 512, 512)],
        pltpu.VMEM((tokens, width), F32),
        pltpu.VMEM((tokens, width), BF16),
        pltpu.VMEM((N_IMG * nz, 512), F32),
        pltpu.VMEM((ngrp, N_IMG, LANES), F32),
        pltpu.VMEM((4, ngrp, N_IMG, LANES), F32),
        pltpu.VMEM((nz, 4 * N_IMG, LANES), BF16),
        pltpu.VMEM((tokens, LANES), F32),
        pltpu.VMEM((tokens, LANES), BF16),
        pltpu.VMEM((2, tokens, LANES), BF16),
        pltpu.VMEM((2, 256, 1024), BF16),
        pltpu.VMEM((4, 2, tokens, 512), BF16),
        pltpu.VMEM((4, 4, tokens, 512), BF16),
        pltpu.VMEM((4, 2, LANES), F32),
        pltpu.VMEM((nz, 2, LANES), F32),
        pltpu.VMEM((2, shard, 256), F32),
        pltpu.VMEM((shard, 256), F32),
        pltpu.VMEM((2, 2, shard * 4 * nz, 128), BF16),
        dma((19,)),
        dma((2,)),
        dma((4 * ngrp - 1,)),
        dma((4 * ngrp - 1,)),
        dma((nz - 1,)),
        dma((nz - 1,)),
        dma((2,)),
        dma((2,)),
        dma((3,)),
        dma((3,)),
        dma((nz - 1,)),
        dma((nz - 1,)),
        dma((2, per)),
        dma((2, per)),
        dma((2, ngrp // 2, per)),
        dma((2, ngrp // 2, per)),
        dma((2,)),
        dma((2,)),
        dma((2,)),
        dma((2,)),
    ]
    out = pl.pallas_call(
        functools.partial(kernel, nz, ngrp),
        out_shape=jax.ShapeDtypeStruct((N_IMG, 2, COLS, 1024), BF16),
        in_specs=[hbm] * 19,
        out_specs=vmem,
        scratch_shapes=scratch,
        compiler_params=pltpu.CompilerParams(
            collective_id=0, has_side_effects=True, vmem_limit_bytes=56 * 1024 * 1024
        ),
    )(
        conditioning,
        mod_weight.T,
        mod_bias.reshape(1, -1),
        hidden.reshape(tokens, width),
        proj_weight.T,
        proj_bias.reshape(1, -1),
        noisy_latent.transpose(0, 1, 3, 2).reshape(128, 128),
        in_weight,
        in_bias.reshape(1, -1),
        norm_gain.reshape(1, -1),
        norm_shift.reshape(1, -1),
        conv_weight,
        conv_bias.reshape(1, -1),
        *consts,
    )
    return out.reshape(N_IMG, 2, 2 * COLS, 512)


def solution(mesh):
    nz = mesh.shape["seq"] // 4
    ngrp = mesh.shape["grp"]
    placed = (
        P(),
        P(None, ("seq", "grp")),
        P(("seq", "grp")),
        P("grp", "seq", None),
        P(),
        P(),
        P("grp", "seq", None, None),
        P(),
        P(),
        P(),
        P(),
        P("seq", None),
        P(),
    )
    return jax.shard_map(
        functools.partial(on_device, nz, ngrp),
        mesh=mesh,
        in_specs=placed,
        out_specs=P("grp", "seq", None, None),
        check_vma=False,
    )
```
